32 devices in a mesh: wide: 8 (over z, x), narrow: 4 (over y, core).
Axes of the slice: x: 2, y: 2, z: 4, core: 2. Of those that a mesh axis runs over, the one named last changes fastest.
Arguments:
- aperture: float32 [64, 128, 128], P(('wide', 'narrow')), may hold values from 0.8 to 2.5
- pressure: float32 [64, 128, 128], P(('wide', 'narrow')), may hold values from -6 to 6
- adj_source: float32 [64, 128, 128], P(('wide', 'narrow')), may hold values from -6 to 6
- trace_weight: float32 [512, 64], P(('wide', 'narrow')), may hold values from 0.2 to 2
- end_device: int32 [512, 2], P(('wide', 'narrow')), may hold values from 0 to 31, as said below
- end_local: int32 [512, 2], P(('wide', 'narrow')), may hold values from 0 to 1
- trace_nodes: int32 [512, 2, 64], P(('wide', 'narrow')), may hold values from 0 to 16383
Outputs:
- aperture_grad: float32 [64, 128, 128], P(('wide', 'narrow'))
- adjoint: float32 [64, 128, 128], P(('wide', 'narrow'))
The draws below stay inside these ranges and needn't reach their ends.
Inputs may be any that keep to these rules, and one draw needn't show every extreme that they name: `end_device`: the two ends of an intersection lie on different devices. Of the ends of the intersections owned by one device, every device holds none or exactly 2. Any two devices are joined by at most 2 intersections over all owners, and some pairs by exactly 2. `trace_nodes`: several trace nodes may share a cell.
All inputs are finite; a program needn't handle non-finite values.
Results may differ from the reference program's by a relative error of at most 0.0022.
Values sent between devices are 32-bit elements; how exact they have to be, the bound alone decides.
No kernel may reach another device: no remote copies, remote signals or barrier semaphores. Data moves between devices by JAX's collectives and lax.ppermute only.
A program may use at most 64 MiB of HBM per device.

```python
import math
import jax
import jax.numpy as jnp

G = 128
TRACE = 64
FR_DEV = 2
SWEEPS = 3
INNER = 8
SPAN = 8
CAP = 2
IX_DEV = 16
FRACTURES = 64
IX = 512
DEVICES = 32


def draw_end_device(key, part):
    cycle_key = jax.random.fold_in(key, 11)
    slot_key = jax.random.fold_in(key, 12)
    flip_key = jax.random.fold_in(key, 13)
    cycle = jax.random.permutation(cycle_key, DEVICES).astype(jnp.int32)
    owner = (jnp.arange(IX, dtype=jnp.int32) // IX_DEV).astype(jnp.int32)
    orders = jax.vmap(lambda k: jax.random.permutation(k, IX_DEV))(jax.random.split(slot_key, DEVICES))
    slot = (orders.reshape(IX).astype(jnp.int32) // CAP).astype(jnp.int32)
    first = cycle[(owner + slot) % DEVICES]
    second = cycle[(owner + SPAN + 2 * slot) % DEVICES]
    flip = jax.random.randint(flip_key, (IX,), 0, 2).astype(jnp.int32)
    end_zero = jnp.where(flip == 1, second, first)
    end_one = jnp.where(flip == 1, first, second)
    return jnp.stack([end_zero, end_one], axis=1).astype(jnp.int32)


def plant(drawn, own_key, low, high):
    spot = [jax.random.randint(jax.random.fold_in(own_key, axis), (), 0, length) for axis, length in enumerate(drawn.shape)]
    widest = drawn.shape.index(max(drawn.shape))
    neighbour = spot[:widest] + [(spot[widest] + 1) % drawn.shape[widest]] + spot[widest + 1:]
    return drawn.at[tuple(spot)].set(low).at[tuple(neighbour)].set(high)


def steps_of(key, dims, pieces, smallest, top_value):
    level = 1.0
    for position, parts in pieces:
        draws = jax.random.uniform(jax.random.fold_in(jax.random.fold_in(key, 6), position), (parts,), jnp.float32, smallest / len(pieces), top_value / len(pieces))
        level = level * jnp.repeat(jnp.exp(draws), dims[position] // parts).reshape((-1,) + (1,) * (len(dims) - 1 - position))
    return level


def normal_values(own_key, dims, spread, reach, cuts=(), held_as=jnp.bfloat16):
    entries = spread * jax.random.normal(own_key, dims, jnp.float32)
    if cuts:
        entries = entries * steps_of(own_key, dims, cuts, -0.22, 0.18)
    return jnp.clip(entries, -reach, reach).astype(held_as)


def setup_inputs(seed: int = 0) -> dict:
    key_of = jax.random.split(jax.random.key(seed), 8)
    return {
        "aperture": jnp.clip(jnp.exp(math.log(2.5) - 1.13943427 * jax.random.uniform(key_of[0], (FRACTURES, G, G), jnp.float32) ** steps_of(key_of[0], (FRACTURES, G, G), ((0, 32),), -0.2, 0.2)), 0.8, 2.5),
        "pressure": normal_values(key_of[1], (FRACTURES, G, G), 1.0, 6.0, ((0, 32),), jnp.float32),
        "adj_source": normal_values(key_of[2], (FRACTURES, G, G), 1.0, 6.0, ((0, 32),), jnp.float32),
        "trace_weight": jnp.clip(jnp.exp(math.log(2.0) - 2.3025851 * jax.random.uniform(key_of[3], (IX, TRACE), jnp.float32) ** steps_of(key_of[3], (IX, TRACE), ((0, 32),), -0.2, 0.2)), 0.2, 2.0),
        "end_device": draw_end_device(jax.random.fold_in(key_of[7], 71), 0),
        "end_local": plant(jax.random.randint(key_of[5], (IX, 2), 0, FR_DEV), jax.random.fold_in(key_of[5], 1), 0, FR_DEV - 1).astype(jnp.int32),
        "trace_nodes": plant(jax.random.randint(key_of[6], (IX, 2, TRACE), 0, G * G), jax.random.fold_in(key_of[6], 1), 0, (G * G) - 1).astype(jnp.int32),
    }


LEAKAGE = 0.25


def neighbours(field, face_x, face_y):
    total = jnp.pad(face_x * field[:, 1:, :], ((0, 0), (0, 1), (0, 0)))
    total = total + jnp.pad(face_x * field[:, :-1, :], ((0, 0), (1, 0), (0, 0)))
    total = total + jnp.pad(face_y * field[:, :, 1:], ((0, 0), (0, 0), (0, 1)))
    total = total + jnp.pad(face_y * field[:, :, :-1], ((0, 0), (0, 0), (1, 0)))
    return total


def face_total(face_x, face_y):
    total = jnp.pad(face_x, ((0, 0), (0, 1), (0, 0))) + jnp.pad(face_x, ((0, 0), (1, 0), (0, 0)))
    return total + jnp.pad(face_y, ((0, 0), (0, 0), (0, 1))) + jnp.pad(face_y, ((0, 0), (0, 0), (1, 0)))


def gradient_of(aperture, pressure, adjoint):
    along_x = (pressure[:, 1:, :] - pressure[:, :-1, :]) * (adjoint[:, 1:, :] - adjoint[:, :-1, :])
    along_y = (pressure[:, :, 1:] - pressure[:, :, :-1]) * (adjoint[:, :, 1:] - adjoint[:, :, :-1])
    return -(aperture * aperture / 8.0) * face_total(along_x, along_y)


def reference(aperture, pressure, adj_source, trace_weight, end_device, end_local, trace_nodes):
    conduct = aperture * aperture * aperture / 12.0
    face_x = (conduct[:, :-1, :] + conduct[:, 1:, :]) * 0.5
    face_y = (conduct[:, :, :-1] + conduct[:, :, 1:]) * 0.5
    fracture = (end_device * FR_DEV + end_local).astype(jnp.int32)
    cells = (fracture[:, :, None] * (G * G) + trace_nodes).astype(jnp.int32).reshape(-1)
    weight_end = jnp.broadcast_to(trace_weight[:, None, :], (IX, 2, TRACE)).reshape(-1)
    total_cells = FRACTURES * G * G
    trace_sum = jnp.zeros((total_cells,), jnp.float32).at[cells].add(weight_end).reshape(FRACTURES, G, G)
    inv_diag = 1.0 / (LEAKAGE + face_total(face_x, face_y) + trace_sum)
    adjoint = adj_source * inv_diag
    for sweep_step in range(SWEEPS):
        values = adjoint.reshape(-1)[cells].reshape(IX, 2, TRACE)
        source = (trace_weight[:, None, :] * values[:, ::-1, :]).reshape(-1)
        coupling = jnp.zeros((total_cells,), jnp.float32).at[cells].add(source).reshape(FRACTURES, G, G)
        forcing = adj_source + coupling
        for inner_step in range(INNER):
            adjoint = (forcing + neighbours(adjoint, face_x, face_y)) * inv_diag
    return gradient_of(aperture, pressure, adjoint), adjoint
```

```python
import functools

import jax
import jax.numpy as jnp
from jax import lax
from jax.experimental import pallas as pl
from jax.experimental.pallas import tpu as pltpu
from jax.sharding import PartitionSpec as P

SWEEPS = 3
INNER = 8
LEAKAGE = 0.25
AXES = ("wide", "narrow")
HIGH = lax.Precision.HIGHEST


def pack_kernel(trace_len, cells_per, dest_ref, local_ref, nodes_ref, weight_ref, out_ref, seen_ref):
    owned = nodes_ref.shape[0]
    devices, _, width = out_ref.shape

    def clear(device, carry):
        seen_ref[device] = 0
        return carry

    lax.fori_loop(0, devices, clear, 0, unroll=8)
    lane = lax.broadcasted_iota(jnp.int32, (1, 1, width), 2)
    out_ref[:, 0:2, :] = jnp.zeros((devices, 2, width), jnp.float32)
    out_ref[:, 2:4, :] = jnp.full((devices, 2, width), -1.0, jnp.float32)

    def place(index, carry):
        ends = [dest_ref[0, index], dest_ref[1, index]]
        weights = weight_ref[pl.ds(index, 1), :]
        for side in range(2):
            target = ends[side]
            rank = seen_ref[target]
            seen_ref[target] = rank + 1
            first = local_ref[side, index] * cells_per + 1
            cells = (nodes_ref[index, side : side + 1, :] + first).astype(jnp.float32)
            row = jnp.concatenate([cells, weights], axis=1)
            out_ref[target, pl.ds(rank, 1), :] = row
            out_ref[target, pl.ds(rank + 2, 1), :] = jnp.full(
                (1, width), ends[1 - side].astype(jnp.float32)
            )
        return carry

    lax.fori_loop(0, owned, place, 0, unroll=True)


def face_parts(conduct, grid_size):
    rows, cols = conduct.shape
    row = lax.broadcasted_iota(jnp.int32, (rows, cols), 0) & (grid_size - 1)
    col = lax.broadcasted_iota(jnp.int32, (rows, cols), 1)
    below = jnp.where(row < grid_size - 1, (conduct + pltpu.roll(conduct, rows - 1, 0)) * 0.5, 0.0)
    above = jnp.where(row > 0, (conduct + pltpu.roll(conduct, 1, 0)) * 0.5, 0.0)
    right = jnp.where(col < cols - 1, (conduct + pltpu.roll(conduct, cols - 1, 1)) * 0.5, 0.0)
    left = jnp.where(col > 0, (conduct + pltpu.roll(conduct, 1, 1)) * 0.5, 0.0)
    return below, above, right, left


def shifted(field):
    rows, cols = field.shape
    return (
        pltpu.roll(field, rows - 1, 0),
        pltpu.roll(field, 1, 0),
        pltpu.roll(field, cols - 1, 1),
        pltpu.roll(field, 1, 1),
    )


def split_pair(values):
    high_part = values.astype(jnp.bfloat16)
    low_part = (values - high_part.astype(jnp.float32)).astype(jnp.bfloat16)
    return high_part, low_part


def scatter(row_hot_ref, col_hot_ref, spread_ref, value_of, devices, width, cols):
    for device in range(devices):
        lanes = slice(device * width, (device + 1) * width)
        high_part, low_part = split_pair(value_of(device))
        hot = col_hot_ref[:, lanes]
        spread_ref[0:cols, lanes] = hot * high_part
        spread_ref[cols : 2 * cols, lanes] = hot * low_part
    both = lax.dot_general(
        row_hot_ref[...], spread_ref[...], (((1,), (1,)), ((), ())), preferred_element_type=jnp.float32
    )
    return both[:, :cols] + both[:, cols:]


def gather(row_hot_ref, col_ref, field, out_ref, devices, width):
    cols = field.shape[1]
    high_part, low_part = split_pair(field.T)
    both = jnp.concatenate([high_part, low_part], axis=0)
    group = 2 if devices % 2 == 0 else 1
    col_ids = lax.broadcasted_iota(jnp.int32, (cols, width), 0)
    for start in range(0, devices, group):
        picked = jnp.dot(
            both,
            row_hot_ref[:, start * width : (start + group) * width],
            preferred_element_type=jnp.float32,
        )
        picked = picked[:cols] + picked[cols:]
        for offset in range(group):
            device = start + offset
            mine = picked[:, offset * width : (offset + 1) * width]
            hit = col_ids == col_ref[device : device + 1, :]
            out_ref[device] = jnp.sum(jnp.where(hit, mine, 0.0), axis=0, keepdims=True)


def first_kernel(
    grid_size, message_ref, aperture_ref, source_ref,
    values_ref, row_hot_ref, col_hot_ref, col_ref, weight_ref, parts_ref, spread_ref,
):
    devices, _, width = message_ref.shape
    trace_len = width // 2
    rows, cols = aperture_ref.shape
    slots = [message_ref[:, rank, :] for rank in range(2)]
    partners = [message_ref[:, 2 + rank, :] for rank in range(2)]
    owner = lax.broadcasted_iota(jnp.int32, (devices, width), 0)
    lane = lax.broadcasted_iota(jnp.int32, (devices, width), 1)
    along = [
        jnp.sum(jnp.where(owner == lane, partners[rank], 0.0), axis=0, keepdims=True)
        for rank in range(2)
    ]
    place_id = owner.astype(jnp.float32)
    ordered = [jnp.zeros((devices, width), jnp.float32) for _ in range(2)]
    for rank in range(2):
        same = [(partners[other] == along[rank]) for other in range(2)]
        before = [owner < lane, owner < lane if rank == 0 else owner <= lane]
        earlier = jnp.where(same[1] & (owner < lane), 1.0, 0.0)
        earlier = earlier + jnp.where(
            same[0] & ((owner < lane) if rank == 0 else (owner <= lane)), 1.0, 0.0
        )
        position = jnp.sum(earlier, axis=0, keepdims=True)
        position = jnp.where(lane[0:1] < devices, position, -1.0)
        for spot in range(2):
            pick = jnp.where((place_id == along[rank]) & (position == float(spot)), 1.0, 0.0)
            ordered[spot] = ordered[spot] + jnp.dot(
                pick[:, :devices], slots[rank], precision=HIGH, preferred_element_type=jnp.float32
            )
    front = lane < trace_len
    cell = jnp.where(front, ordered[0], pltpu.roll(ordered[1], trace_len, 1)).astype(jnp.int32) - 1
    weight_ref[...] = jnp.where(front, pltpu.roll(ordered[0], trace_len, 1), ordered[1])
    row = cell >> (grid_size.bit_length() - 1)
    col = cell & (grid_size - 1)
    col_ref[...] = col
    row_ids = lax.broadcasted_iota(jnp.int32, (rows, width), 0)
    col_ids = lax.broadcasted_iota(jnp.int32, (cols, width), 0)
    for device in range(devices):
        lanes = slice(device * width, (device + 1) * width)
        row_hot_ref[:, lanes] = jnp.where(row_ids == row[device : device + 1], 1.0, 0.0).astype(jnp.bfloat16)
        col_hot_ref[:, lanes] = jnp.where(col_ids == col[device : device + 1], 1.0, 0.0).astype(jnp.bfloat16)
    trace_sum = scatter(
        row_hot_ref, col_hot_ref, spread_ref, lambda device: weight_ref[device : device + 1, :], devices, width, cols
    )
    aperture = aperture_ref[...]
    faces = face_parts(aperture * aperture * aperture / 12.0, grid_size)
    inv_diag = 1.0 / (LEAKAGE + (faces[0] + faces[1] + faces[2] + faces[3]) + trace_sum)
    for index in range(4):
        parts_ref[index] = faces[index] * inv_diag
    parts_ref[4] = inv_diag
    adjoint = source_ref[...] * inv_diag
    parts_ref[5] = adjoint
    gather(row_hot_ref, col_ref, adjoint, values_ref, devices, width)


def relax(arrived_ref, row_hot_ref, col_hot_ref, weight_ref, parts_ref, start, source_ref, spread_ref):
    devices, _, width = arrived_ref.shape
    cols = source_ref.shape[1]
    coupling = scatter(
        row_hot_ref, col_hot_ref, spread_ref,
        lambda device: weight_ref[device : device + 1, :] * arrived_ref[device], devices, width, cols,
    )
    forcing = (source_ref[...] + coupling) * parts_ref[4]
    adjoint = start
    for _ in range(INNER):
        below, above, right, left = shifted(adjoint)
        adjoint = (
            forcing + (parts_ref[0] * below + parts_ref[1] * above)
            + (parts_ref[2] * right + parts_ref[3] * left)
        )
    return adjoint


def sweep_kernel(
    arrived_ref, row_hot_ref, col_hot_ref, col_ref, weight_ref, parts_ref, start_ref, source_ref,
    values_ref, adjoint_ref, spread_ref,
):
    devices, _, width = arrived_ref.shape
    adjoint = relax(
        arrived_ref, row_hot_ref, col_hot_ref, weight_ref, parts_ref, start_ref[...], source_ref, spread_ref
    )
    adjoint_ref[...] = adjoint
    gather(row_hot_ref, col_ref, adjoint, values_ref, devices, width)


def last_kernel(
    grid_size, arrived_ref, row_hot_ref, col_hot_ref, weight_ref, parts_ref, start_ref, source_ref,
    aperture_ref, pressure_ref, gradient_ref, adjoint_ref, spread_ref,
):
    adjoint = relax(
        arrived_ref, row_hot_ref, col_hot_ref, weight_ref, parts_ref, start_ref[...], source_ref, spread_ref
    )
    adjoint_ref[...] = adjoint
    pressure = pressure_ref[...]
    rows, cols = adjoint.shape
    row = lax.broadcasted_iota(jnp.int32, (rows, cols), 0) & (grid_size - 1)
    col = lax.broadcasted_iota(jnp.int32, (rows, cols), 1)
    inside = (row < grid_size - 1, row > 0, col < cols - 1, col > 0)
    total = jnp.zeros((rows, cols), jnp.float32)
    for keep, near_pressure, near_adjoint in zip(inside, shifted(pressure), shifted(adjoint), strict=True):
        total = total + jnp.where(keep, (pressure - near_pressure) * (adjoint - near_adjoint), 0.0)
    aperture = aperture_ref[...]
    gradient_ref[...] = -(aperture * aperture / 8.0) * total


def body(aperture, pressure, adj_source, trace_weight, end_device, end_local, trace_nodes):
    frac_count, grid_size, _ = aperture.shape
    owned_count, trace_len = trace_weight.shape
    device_count = lax.axis_size(AXES)
    rows, cols, width = frac_count * grid_size, grid_size, 2 * trace_len
    nodes = device_count * width
    in_vmem = pl.BlockSpec(memory_space=pltpu.VMEM)
    in_smem = pl.BlockSpec(memory_space=pltpu.SMEM)
    params = pltpu.CompilerParams(vmem_limit_bytes=(8 << 20) + nodes * 2560)
    spread = pltpu.VMEM((2 * cols, nodes), jnp.bfloat16)

    def flat(field):
        return field.reshape(rows, cols)

    def vmem(*arrays):
        return [pltpu.with_memory_space_constraint(array, pltpu.VMEM) for array in arrays]

    def exchange(values):
        return lax.all_to_all(values, AXES, split_axis=0, concat_axis=0, tiled=True)

    message = pl.pallas_call(
        functools.partial(pack_kernel, trace_len, grid_size * grid_size),
        out_shape=pltpu.VMEM((device_count, 4, width), jnp.float32),
        in_specs=[in_smem, in_smem, in_vmem, in_vmem],
        out_specs=in_vmem,
        scratch_shapes=[pltpu.SMEM((device_count,), jnp.int32)],
        compiler_params=params,
        name="pack_ends",
    )(end_device.T, end_local.T, trace_nodes, trace_weight)
    values_shape = pltpu.VMEM((device_count, 1, width), jnp.float32)
    field_shape = pltpu.VMEM((rows, cols), jnp.float32)
    values, row_hot, col_hot, col, weight, parts = pl.pallas_call(
        functools.partial(first_kernel, grid_size),
        out_shape=[
            values_shape,
            pltpu.VMEM((rows, nodes), jnp.bfloat16),
            pltpu.VMEM((cols, nodes), jnp.bfloat16),
            pltpu.VMEM((device_count, width), jnp.int32),
            pltpu.VMEM((device_count, width), jnp.float32),
            pltpu.VMEM((6, rows, cols), jnp.float32),
        ],
        in_specs=[in_vmem] * 3,
        out_specs=[in_vmem] * 6,
        scratch_shapes=[spread],
        compiler_params=params,
        name="first_values",
    )(*vmem(exchange(message)), flat(aperture), flat(adj_source))
    adjoint = parts[5]
    for _ in range(SWEEPS - 1):
        values, adjoint = pl.pallas_call(
            sweep_kernel,
            out_shape=[values_shape, field_shape],
            in_specs=[in_vmem] * 8,
            out_specs=[in_vmem] * 2,
            scratch_shapes=[spread],
            compiler_params=params,
            name="sweep",
        )(*vmem(exchange(values), row_hot, col_hot, col, weight, parts, adjoint), flat(adj_source))
    gradient, adjoint = pl.pallas_call(
        functools.partial(last_kernel, grid_size),
        out_shape=[jax.ShapeDtypeStruct((rows, cols), jnp.float32)] * 2,
        in_specs=[in_vmem] * 9,
        out_specs=[in_vmem] * 2,
        scratch_shapes=[spread],
        compiler_params=params,
        name="last_sweep",
    )(
        *vmem(exchange(values), row_hot, col_hot, weight, parts, adjoint),
        flat(adj_source), flat(aperture), flat(pressure),
    )
    return gradient.reshape(aperture.shape), adjoint.reshape(aperture.shape)


def solution(mesh):
    fields, pairs = P(AXES, None, None), P(AXES, None)
    return jax.shard_map(
        body,
        mesh=mesh,
        in_specs=(fields, fields, fields, pairs, pairs, pairs, fields),
        out_specs=(fields, fields),
        check_vma=False,
    )
```

```python
import functools

import jax
import jax.numpy as jnp
from jax import lax
from jax.experimental import pallas as pl
from jax.experimental.pallas import tpu as pltpu
from jax.sharding import PartitionSpec as P

SWEEPS = 3
INNER = 8
LEAKAGE = 0.25
AXES = ("wide", "narrow")
HIGH = lax.Precision.HIGHEST


def pack_kernel(
    cells_per, dest_hbm, local_hbm, nodes_hbm, weight_hbm, aperture_hbm, source_hbm, pressure_hbm,
    out_ref, aperture_ref, source_ref, pressure_ref,
    dest_ref, local_ref, nodes_ref, weight_ref, seen_ref, small_sems, large_sems,
):
    owned = nodes_ref.shape[0]
    devices, _, width = out_ref.shape
    small = [
        pltpu.make_async_copy(source, target, small_sems.at[index])
        for index, (source, target) in enumerate(
            ((dest_hbm, dest_ref), (local_hbm, local_ref), (nodes_hbm, nodes_ref), (weight_hbm, weight_ref))
        )
    ]
    large = [
        pltpu.make_async_copy(source, target, large_sems.at[index])
        for index, (source, target) in enumerate(
            ((aperture_hbm, aperture_ref), (source_hbm, source_ref), (pressure_hbm, pressure_ref))
        )
    ]
    for copy in small + large:
        copy.start()

    def clear(device, carry):
        seen_ref[device] = 0
        return carry

    lax.fori_loop(0, devices, clear, 0, unroll=8)
    out_ref[:, 0:2, :] = jnp.zeros((devices, 2, width), jnp.float32)
    out_ref[:, 2:4, :] = jnp.full((devices, 2, width), -1.0, jnp.float32)
    for copy in small:
        copy.wait()

    def place(index, carry):
        ends = [dest_ref[0, index], dest_ref[1, index]]
        weights = weight_ref[pl.ds(index, 1), :]
        for side in range(2):
            target = ends[side]
            rank = seen_ref[target]
            seen_ref[target] = rank + 1
            first = local_ref[side, index] * cells_per + 1
            cells = (nodes_ref[index, side : side + 1, :] + first).astype(jnp.float32)
            out_ref[target, pl.ds(rank, 1), :] = jnp.concatenate([cells, weights], axis=1)
            out_ref[target, pl.ds(rank + 2, 1), :] = jnp.full(
                (1, width), ends[1 - side].astype(jnp.float32)
            )
        return carry

    lax.fori_loop(0, owned, place, 0, unroll=True)
    for copy in large:
        copy.wait()


def face_parts(conduct, grid_size):
    rows, cols = conduct.shape
    row = lax.broadcasted_iota(jnp.int32, (rows, cols), 0) & (grid_size - 1)
    col = lax.broadcasted_iota(jnp.int32, (rows, cols), 1)
    below = jnp.where(row < grid_size - 1, (conduct + pltpu.roll(conduct, rows - 1, 0)) * 0.5, 0.0)
    above = jnp.where(row > 0, (conduct + pltpu.roll(conduct, 1, 0)) * 0.5, 0.0)
    right = jnp.where(col < cols - 1, (conduct + pltpu.roll(conduct, cols - 1, 1)) * 0.5, 0.0)
    left = jnp.where(col > 0, (conduct + pltpu.roll(conduct, 1, 1)) * 0.5, 0.0)
    return below, above, right, left


def shifted(field):
    rows, cols = field.shape
    return (
        pltpu.roll(field, rows - 1, 0),
        pltpu.roll(field, 1, 0),
        pltpu.roll(field, cols - 1, 1),
        pltpu.roll(field, 1, 1),
    )


def split_pair(values):
    high_part = values.astype(jnp.bfloat16)
    low_part = (values - high_part.astype(jnp.float32)).astype(jnp.bfloat16)
    return high_part, low_part


def scatter(row_hot_ref, col_hot_ref, spread_ref, value_of, devices, width, cols):
    for device in range(devices):
        lanes = slice(device * width, (device + 1) * width)
        high_part, low_part = split_pair(value_of(device))
        hot = col_hot_ref[:, lanes]
        spread_ref[0:cols, lanes] = hot * high_part
        spread_ref[cols : 2 * cols, lanes] = hot * low_part
    both = lax.dot_general(
        row_hot_ref[...], spread_ref[...], (((1,), (1,)), ((), ())), preferred_element_type=jnp.float32
    )
    return both[:, :cols] + both[:, cols:]


def gather(row_hot_ref, col_ref, field, out_ref, devices, width):
    cols = field.shape[1]
    high_part, low_part = split_pair(field.T)
    both = jnp.concatenate([high_part, low_part], axis=0)
    group = 2 if devices % 2 == 0 else 1
    col_ids = lax.broadcasted_iota(jnp.int32, (cols, width), 0)
    for start in range(0, devices, group):
        picked = jnp.dot(
            both,
            row_hot_ref[:, start * width : (start + group) * width],
            preferred_element_type=jnp.float32,
        )
        picked = picked[:cols] + picked[cols:]
        for offset in range(group):
            device = start + offset
            mine = picked[:, offset * width : (offset + 1) * width]
            hit = col_ids == col_ref[device : device + 1, :]
            out_ref[device] = jnp.sum(jnp.where(hit, mine, 0.0), axis=0, keepdims=True)


def first_kernel(
    grid_size, message_ref, aperture_ref, source_ref,
    values_ref, row_hot_ref, col_hot_ref, col_ref, weight_ref, parts_ref, adjoint_ref, spread_ref,
):
    devices, _, width = message_ref.shape
    trace_len = width // 2
    rows, cols = aperture_ref.shape
    slots = [message_ref[:, rank, :] for rank in range(2)]
    partners = [message_ref[:, 2 + rank, :] for rank in range(2)]
    owner = lax.broadcasted_iota(jnp.int32, (devices, width), 0)
    lane = lax.broadcasted_iota(jnp.int32, (devices, width), 1)
    along = [
        jnp.sum(jnp.where(owner == lane, partners[rank], 0.0), axis=0, keepdims=True)
        for rank in range(2)
    ]
    place_id = owner.astype(jnp.float32)
    ordered = [jnp.zeros((devices, width), jnp.float32) for _ in range(2)]
    for rank in range(2):
        same = [(partners[other] == along[rank]) for other in range(2)]
        earlier = jnp.where(same[1] & (owner < lane), 1.0, 0.0)
        earlier = earlier + jnp.where(
            same[0] & ((owner < lane) if rank == 0 else (owner <= lane)), 1.0, 0.0
        )
        position = jnp.sum(earlier, axis=0, keepdims=True)
        position = jnp.where(lane[0:1] < devices, position, -1.0)
        for spot in range(2):
            pick = jnp.where((place_id == along[rank]) & (position == float(spot)), 1.0, 0.0)
            ordered[spot] = ordered[spot] + jnp.dot(
                pick[:, :devices], slots[rank], precision=HIGH, preferred_element_type=jnp.float32
            )
    front = lane < trace_len
    cell = jnp.where(front, ordered[0], pltpu.roll(ordered[1], trace_len, 1)).astype(jnp.int32) - 1
    weight_ref[...] = jnp.where(front, pltpu.roll(ordered[0], trace_len, 1), ordered[1])
    row = cell >> (grid_size.bit_length() - 1)
    col = cell & (grid_size - 1)
    col_ref[...] = col
    row_ids = lax.broadcasted_iota(jnp.int32, (rows, width), 0)
    col_ids = lax.broadcasted_iota(jnp.int32, (cols, width), 0)
    for device in range(devices):
        lanes = slice(device * width, (device + 1) * width)
        row_hot_ref[:, lanes] = jnp.where(row_ids == row[device : device + 1], 1.0, 0.0).astype(jnp.bfloat16)
        col_hot_ref[:, lanes] = jnp.where(col_ids == col[device : device + 1], 1.0, 0.0).astype(jnp.bfloat16)
    trace_sum = scatter(
        row_hot_ref, col_hot_ref, spread_ref, lambda device: weight_ref[device : device + 1, :], devices, width, cols
    )
    aperture = aperture_ref[...]
    faces = face_parts(aperture * aperture * aperture / 12.0, grid_size)
    inv_diag = 1.0 / (LEAKAGE + (faces[0] + faces[1] + faces[2] + faces[3]) + trace_sum)
    for index in range(4):
        parts_ref[index] = faces[index] * inv_diag
    parts_ref[4] = inv_diag
    adjoint = source_ref[...] * inv_diag
    adjoint_ref[...] = adjoint
    gather(row_hot_ref, col_ref, adjoint, values_ref, devices, width)


def relax(arrived_ref, row_hot_ref, col_hot_ref, weight_ref, parts_ref, start, source_ref, spread_ref):
    devices, _, width = arrived_ref.shape
    cols = source_ref.shape[1]
    coupling = scatter(
        row_hot_ref, col_hot_ref, spread_ref,
        lambda device: weight_ref[device : device + 1, :] * arrived_ref[device], devices, width, cols,
    )
    forcing = (source_ref[...] + coupling) * parts_ref[4]
    adjoint = start
    for _ in range(INNER):
        below, above, right, left = shifted(adjoint)
        adjoint = (
            forcing + (parts_ref[0] * below + parts_ref[1] * above)
            + (parts_ref[2] * right + parts_ref[3] * left)
        )
    return adjoint


def sweep_kernel(
    arrived_ref, row_hot_ref, col_hot_ref, col_ref, weight_ref, parts_ref, start_ref, source_ref,
    values_ref, adjoint_ref, spread_ref,
):
    devices, _, width = arrived_ref.shape
    adjoint = relax(
        arrived_ref, row_hot_ref, col_hot_ref, weight_ref, parts_ref, start_ref[...], source_ref, spread_ref
    )
    adjoint_ref[...] = adjoint
    gather(row_hot_ref, col_ref, adjoint, values_ref, devices, width)


def last_kernel(
    grid_size, arrived_ref, row_hot_ref, col_hot_ref, weight_ref, parts_ref, start_ref, source_ref,
    aperture_ref, pressure_ref, gradient_ref, adjoint_ref, spread_ref,
):
    adjoint = relax(
        arrived_ref, row_hot_ref, col_hot_ref, weight_ref, parts_ref, start_ref[...], source_ref, spread_ref
    )
    adjoint_ref[...] = adjoint
    pressure = pressure_ref[...]
    rows, cols = adjoint.shape
    row = lax.broadcasted_iota(jnp.int32, (rows, cols), 0) & (grid_size - 1)
    col = lax.broadcasted_iota(jnp.int32, (rows, cols), 1)
    inside = (row < grid_size - 1, row > 0, col < cols - 1, col > 0)
    total = jnp.zeros((rows, cols), jnp.float32)
    for keep, near_pressure, near_adjoint in zip(inside, shifted(pressure), shifted(adjoint), strict=True):
        total = total + jnp.where(keep, (pressure - near_pressure) * (adjoint - near_adjoint), 0.0)
    aperture = aperture_ref[...]
    gradient_ref[...] = -(aperture * aperture / 8.0) * total


def body(aperture, pressure, adj_source, trace_weight, end_device, end_local, trace_nodes):
    frac_count, grid_size, _ = aperture.shape
    owned_count, trace_len = trace_weight.shape
    device_count = lax.axis_size(AXES)
    rows, cols, width = frac_count * grid_size, grid_size, 2 * trace_len
    nodes = device_count * width
    in_vmem = pl.BlockSpec(memory_space=pltpu.VMEM)
    in_smem = pl.BlockSpec(memory_space=pltpu.SMEM)
    params = pltpu.CompilerParams(vmem_limit_bytes=(8 << 20) + nodes * 2560)
    spread = pltpu.VMEM((2 * cols, nodes), jnp.bfloat16)

    def flat(field):
        return field.reshape(rows, cols)

    def vmem(*arrays):
        return [pltpu.with_memory_space_constraint(array, pltpu.VMEM) for array in arrays]

    def exchange(values):
        return lax.all_to_all(values, AXES, split_axis=0, concat_axis=0, tiled=True)

    field_shape = pltpu.VMEM((rows, cols), jnp.float32)
    in_hbm = pl.BlockSpec(memory_space=pltpu.HBM)
    arguments = (
        end_device.T, end_local.T, trace_nodes, trace_weight, flat(aperture), flat(adj_source), flat(pressure)
    )
    message, aperture_here, source_here, pressure_here = pl.pallas_call(
        functools.partial(pack_kernel, grid_size * grid_size),
        out_shape=[pltpu.VMEM((device_count, 4, width), jnp.float32)] + [field_shape] * 3,
        in_specs=[in_hbm] * 7,
        out_specs=[in_vmem] * 4,
        scratch_shapes=[
            pltpu.SMEM((2, owned_count), jnp.int32),
            pltpu.SMEM((2, owned_count), jnp.int32),
            pltpu.VMEM(trace_nodes.shape, jnp.int32),
            pltpu.VMEM(trace_weight.shape, jnp.float32),
            pltpu.SMEM((device_count,), jnp.int32),
            pltpu.SemaphoreType.DMA((4,)),
            pltpu.SemaphoreType.DMA((3,)),
        ],
        compiler_params=params,
        name="pack_ends",
    )(*[pltpu.with_memory_space_constraint(array, pltpu.HBM) for array in arguments])
    values_shape = pltpu.VMEM((device_count, 1, width), jnp.float32)
    values, row_hot, col_hot, col, weight, parts, adjoint = pl.pallas_call(
        functools.partial(first_kernel, grid_size),
        out_shape=[
            values_shape,
            pltpu.VMEM((rows, nodes), jnp.bfloat16),
            pltpu.VMEM((cols, nodes), jnp.bfloat16),
            pltpu.VMEM((device_count, width), jnp.int32),
            pltpu.VMEM((device_count, width), jnp.float32),
            pltpu.VMEM((5, rows, cols), jnp.float32),
            field_shape,
        ],
        in_specs=[in_vmem] * 3,
        out_specs=[in_vmem] * 7,
        scratch_shapes=[spread],
        compiler_params=params,
        name="first_values",
    )(*vmem(exchange(message), aperture_here, source_here))
    for _ in range(SWEEPS - 1):
        values, adjoint = pl.pallas_call(
            sweep_kernel,
            out_shape=[values_shape, field_shape],
            in_specs=[in_vmem] * 8,
            out_specs=[in_vmem] * 2,
            scratch_shapes=[spread],
            compiler_params=params,
            name="sweep",
        )(*vmem(exchange(values), row_hot, col_hot, col, weight, parts, adjoint, source_here))
    gradient, adjoint = pl.pallas_call(
        functools.partial(last_kernel, grid_size),
        out_shape=[jax.ShapeDtypeStruct((rows, cols), jnp.float32)] * 2,
        in_specs=[in_vmem] * 9,
        out_specs=[in_vmem] * 2,
        scratch_shapes=[spread],
        compiler_params=params,
        name="last_sweep",
    )(
        *vmem(
            exchange(values), row_hot, col_hot, weight, parts, adjoint,
            source_here, aperture_here, pressure_here,
        )
    )
    return gradient.reshape(aperture.shape), adjoint.reshape(aperture.shape)


def solution(mesh):
    fields, pairs = P(AXES, None, None), P(AXES, None)
    return jax.shard_map(
        body,
        mesh=mesh,
        in_specs=(fields, fields, fields, pairs, pairs, pairs, fields),
        out_specs=(fields, fields),
        check_vma=False,
    )
```

```python
import functools
import math

import jax
import jax.numpy as jnp
from jax import lax
from jax.experimental import pallas as pl
from jax.experimental.pallas import tpu as pltpu
from jax.sharding import PartitionSpec as P

SWEEPS = 3
INNER = 8
LEAKAGE = 0.25
AXES = ("wide", "narrow")
HIGH = lax.Precision.HIGHEST


def pack_kernel(
    cells_per, dest_hbm, local_hbm, nodes_hbm, weight_hbm, aperture_hbm, source_hbm, pressure_hbm,
    out_ref, aperture_ref, source_ref, pressure_ref,
    dest_ref, local_ref, nodes_ref, weight_ref, seen_ref, small_sems, large_sems,
):
    owned = nodes_ref.shape[0]
    devices, _, width = out_ref.shape
    small = [
        pltpu.make_async_copy(source, target, small_sems.at[index])
        for index, (source, target) in enumerate(
            ((dest_hbm, dest_ref), (local_hbm, local_ref), (nodes_hbm, nodes_ref), (weight_hbm, weight_ref))
        )
    ]
    large = [
        pltpu.make_async_copy(source, target, large_sems.at[index])
        for index, (source, target) in enumerate(
            ((aperture_hbm, aperture_ref), (source_hbm, source_ref), (pressure_hbm, pressure_ref))
        )
    ]
    for copy in small + large:
        copy.start()

    def clear(device, carry):
        seen_ref[device] = 0
        return carry

    lax.fori_loop(0, devices, clear, 0, unroll=8)
    out_ref[:, 0:2, :] = jnp.zeros((devices, 2, width), jnp.float32)
    out_ref[:, 2:4, :] = jnp.full((devices, 2, width), -1.0, jnp.float32)
    for copy in small:
        copy.wait()

    def place(index, carry):
        ends = [dest_ref[0, index], dest_ref[1, index]]
        weights = weight_ref[pl.ds(index, 1), :]
        for side in range(2):
            target = ends[side]
            rank = seen_ref[target]
            seen_ref[target] = rank + 1
            first = local_ref[side, index] * cells_per + 1
            cells = (nodes_ref[index, side : side + 1, :] + first).astype(jnp.float32)
            out_ref[target, pl.ds(rank, 1), :] = jnp.concatenate([cells, weights], axis=1)
            out_ref[target, pl.ds(rank + 2, 1), :] = jnp.full(
                (1, width), ends[1 - side].astype(jnp.float32)
            )
        return carry

    lax.fori_loop(0, owned, place, 0, unroll=True)
    for copy in large:
        copy.wait()


def face_parts(conduct, grid_size):
    rows, cols = conduct.shape
    row = lax.broadcasted_iota(jnp.int32, (rows, cols), 0) & (grid_size - 1)
    col = lax.broadcasted_iota(jnp.int32, (rows, cols), 1)
    below = jnp.where(row < grid_size - 1, (conduct + pltpu.roll(conduct, rows - 1, 0)) * 0.5, 0.0)
    above = jnp.where(row > 0, (conduct + pltpu.roll(conduct, 1, 0)) * 0.5, 0.0)
    right = jnp.where(col < cols - 1, (conduct + pltpu.roll(conduct, cols - 1, 1)) * 0.5, 0.0)
    left = jnp.where(col > 0, (conduct + pltpu.roll(conduct, 1, 1)) * 0.5, 0.0)
    return below, above, right, left


def shifted(field):
    rows, cols = field.shape
    return (
        pltpu.roll(field, rows - 1, 0),
        pltpu.roll(field, 1, 0),
        pltpu.roll(field, cols - 1, 1),
        pltpu.roll(field, 1, 1),
    )


def split_pair(values):
    high_part = values.astype(jnp.bfloat16)
    low_part = (values - high_part.astype(jnp.float32)).astype(jnp.bfloat16)
    return jnp.concatenate([high_part, low_part], axis=1)


def over_blocks(count_ref, blocks, work):
    per_block = count_ref.shape[0] // blocks
    work(0)
    if blocks > 1:
        needed = lax.div(count_ref[0, 0] + (per_block - 1), per_block)

        def step(block, carry):
            work(block)
            return carry

        lax.fori_loop(1, needed, step, 0)


def spread_dot(row_hot_ref, col_hot_ref, total_ref, value_ref, block):
    _, cols, lanes = col_hot_ref.shape
    width = value_ref.shape[2] // 2
    group = 2
    total = None
    for start in range(0, lanes // width, group):
        parts = [[], []]
        for device in range(start, start + group):
            hot = col_hot_ref[block, :, device * width : (device + 1) * width]
            value = value_ref[block, device : device + 1, :]
            for index in range(2):
                parts[index].append(hot * value[:, index * width : (index + 1) * width])
        right = jnp.concatenate([jnp.concatenate(part, axis=1) for part in parts], axis=0)
        product = lax.dot_general(
            row_hot_ref[block, :, start * width : (start + group) * width],
            right,
            (((1,), (1,)), ((), ())),
            preferred_element_type=jnp.float32,
        )
        total = product if total is None else total + product
    total = total[:, :cols] + total[:, cols:]
    if isinstance(block, int):
        total_ref[...] = total
    else:
        total_ref[...] += total


def gather(row_hot_ref, col_ref, both_ref, picked_ref, block):
    lanes = row_hot_ref.shape[2]
    _, per_block, width = picked_ref.shape
    cols = both_ref.shape[0] // 2
    group = 2
    col_ids = lax.broadcasted_iota(jnp.int32, (cols, width), 0)
    both = both_ref[...]
    for start in range(0, per_block, group):
        picked = jnp.dot(
            both,
            row_hot_ref[block, :, start * width : (start + group) * width],
            preferred_element_type=jnp.float32,
        )
        picked = picked[:cols] + picked[cols:]
        for offset in range(group):
            device = start + offset
            mine = picked[:, offset * width : (offset + 1) * width]
            hit = col_ids == col_ref[block, device : device + 1, :]
            picked_ref[block, device : device + 1, :] = jnp.sum(
                jnp.where(hit, mine, 0.0), axis=0, keepdims=True
            )


def send_values(adjoint, row_hot_ref, col_ref, count_ref, order_ref, both_ref, picked_ref, values_ref):
    blocks, per_block, width = picked_ref.shape
    devices = blocks * per_block
    turned = split_pair(adjoint.T)
    rows = adjoint.shape[0]
    both_ref[...] = jnp.concatenate([turned[:, :rows], turned[:, rows:]], axis=0)
    if blocks > 1:
        picked_ref[1:] = jnp.zeros((blocks - 1, per_block, width), jnp.float32)
    over_blocks(count_ref, blocks, lambda block: gather(row_hot_ref, col_ref, both_ref, picked_ref, block))
    picked = split_pair(picked_ref[...].reshape(devices, width))
    sent = jnp.dot(order_ref[1, :, :devices], picked, preferred_element_type=jnp.float32)
    values_ref[:, 0, :] = sent[:, :width] + sent[:, width:]


def first_kernel(
    grid_size, message_ref, aperture_ref, source_ref,
    values_ref, row_hot_ref, col_hot_ref, col_ref, weight_ref, count_ref, order_ref, parts_ref, adjoint_ref,
    row_ref, value_ref, total_ref, both_ref, picked_ref,
):
    devices, _, width = message_ref.shape
    trace_len = width // 2
    blocks, per_block, _ = col_ref.shape
    rows, cols = aperture_ref.shape
    slots = [message_ref[:, rank, :] for rank in range(2)]
    partners = [message_ref[:, 2 + rank, :] for rank in range(2)]
    down = lax.broadcasted_iota(jnp.int32, (devices, width), 0)
    along = lax.broadcasted_iota(jnp.int32, (devices, width), 1)
    partner_along = [
        jnp.sum(jnp.where(down == along, partners[rank], 0.0), axis=0, keepdims=True) for rank in range(2)
    ]
    device_id = down.astype(jnp.float32)
    ordered = [jnp.zeros((devices, width), jnp.float32) for _ in range(2)]
    for rank in range(2):
        same = [partners[other] == partner_along[rank] for other in range(2)]
        ahead = (down < along) if rank == 0 else (down <= along)
        earlier = jnp.where(same[0] & ahead, 1.0, 0.0) + jnp.where(same[1] & (down < along), 1.0, 0.0)
        position = jnp.sum(earlier, axis=0, keepdims=True)
        for spot in range(2):
            pick = jnp.where((device_id == partner_along[rank]) & (position == float(spot)), 1.0, 0.0)
            ordered[spot] = ordered[spot] + jnp.dot(
                pick[:, :devices], slots[rank], precision=HIGH, preferred_element_type=jnp.float32
            )
    front = along < trace_len
    cell = jnp.where(front, ordered[0], pltpu.roll(ordered[1], trace_len, 1)).astype(jnp.int32) - 1
    weight = jnp.where(front, pltpu.roll(ordered[0], trace_len, 1), ordered[1])
    weight_ref[...] = weight
    used_down = jnp.max(jnp.where(cell >= 0, 1.0, 0.0), axis=1, keepdims=True)
    used_along = jnp.sum(jnp.where(down == along, used_down, 0.0), axis=0, keepdims=True)
    place_along = jnp.sum(jnp.where(down < along, used_down, 0.0), axis=0, keepdims=True)
    place_down = jnp.sum(jnp.where(along < down, used_along, 0.0), axis=1, keepdims=True)
    count_ref[...] = jnp.broadcast_to(jnp.sum(used_down, axis=0, keepdims=True), count_ref.shape).astype(jnp.int32)
    order_ref[0] = jnp.where((device_id == place_along) & (used_along > 0.5), 1.0, 0.0).astype(jnp.bfloat16)
    order_ref[1] = jnp.where((along.astype(jnp.float32) == place_down) & (used_down > 0.5), 1.0, 0.0).astype(
        jnp.bfloat16
    )
    row = (cell >> (grid_size.bit_length() - 1)).astype(jnp.float32).astype(jnp.bfloat16)
    col = (cell & (grid_size - 1)).astype(jnp.float32).astype(jnp.bfloat16)
    packed = jnp.dot(
        order_ref[0, :, :devices],
        jnp.concatenate([row, col, split_pair(weight)], axis=1),
        preferred_element_type=jnp.float32,
    )
    row_ref[...] = packed[:, :width].astype(jnp.bfloat16).reshape(row_ref.shape)
    col_ref[...] = packed[:, width : 2 * width].astype(jnp.int32).reshape(col_ref.shape)
    value_ref[...] = packed[:, 2 * width :].astype(jnp.bfloat16).reshape(value_ref.shape)
    cell_ids = lax.broadcasted_iota(jnp.int32, (rows, width), 0).astype(jnp.float32).astype(jnp.bfloat16)
    one, zero = jnp.ones((), jnp.bfloat16), jnp.zeros((), jnp.bfloat16)

    def build(block):
        block_cols = col_ref[block].astype(jnp.float32).astype(jnp.bfloat16)
        block_rows = row_ref[block]
        for device in range(per_block):
            lanes = slice(device * width, (device + 1) * width)
            row_hot_ref[block, :, lanes] = jnp.where(cell_ids == block_rows[device : device + 1], one, zero)
            col_hot_ref[block, :, lanes] = jnp.where(
                cell_ids[:cols] == block_cols[device : device + 1], one, zero
            )
        spread_dot(row_hot_ref, col_hot_ref, total_ref, value_ref, block)

    over_blocks(count_ref, blocks, build)
    aperture = aperture_ref[...]
    faces = face_parts(aperture * aperture * aperture / 12.0, grid_size)
    inv_diag = 1.0 / (LEAKAGE + (faces[0] + faces[1] + faces[2] + faces[3]) + total_ref[...])
    for index in range(4):
        parts_ref[index] = faces[index] * inv_diag
    parts_ref[4] = inv_diag
    adjoint = source_ref[...] * inv_diag
    adjoint_ref[...] = adjoint
    send_values(adjoint, row_hot_ref, col_ref, count_ref, order_ref, both_ref, picked_ref, values_ref)


def relax(
    arrived_ref, row_hot_ref, col_hot_ref, weight_ref, count_ref, order_ref, parts_ref, start_ref, source_ref,
    value_ref, total_ref,
):
    blocks = value_ref.shape[0]
    devices = arrived_ref.shape[0]
    terms = split_pair(weight_ref[...] * arrived_ref[:, 0, :])
    placed = jnp.dot(order_ref[0, :, :devices], terms, preferred_element_type=jnp.float32)
    value_ref[...] = placed.astype(jnp.bfloat16).reshape(value_ref.shape)
    over_blocks(
        count_ref, blocks, lambda block: spread_dot(row_hot_ref, col_hot_ref, total_ref, value_ref, block)
    )
    forcing = (source_ref[...] + total_ref[...]) * parts_ref[4]
    adjoint = start_ref[...]
    for _ in range(INNER):
        below, above, right, left = shifted(adjoint)
        adjoint = (
            forcing + (parts_ref[0] * below + parts_ref[1] * above)
            + (parts_ref[2] * right + parts_ref[3] * left)
        )
    return adjoint


def sweep_kernel(
    arrived_ref, row_hot_ref, col_hot_ref, col_ref, weight_ref, count_ref, order_ref, parts_ref, start_ref,
    source_ref, values_ref, adjoint_ref, value_ref, total_ref, both_ref, picked_ref,
):
    adjoint = relax(
        arrived_ref, row_hot_ref, col_hot_ref, weight_ref, count_ref, order_ref, parts_ref, start_ref, source_ref,
        value_ref, total_ref,
    )
    adjoint_ref[...] = adjoint
    send_values(adjoint, row_hot_ref, col_ref, count_ref, order_ref, both_ref, picked_ref, values_ref)


def last_kernel(
    grid_size, arrived_ref, row_hot_ref, col_hot_ref, weight_ref, count_ref, order_ref, parts_ref, start_ref,
    source_ref, aperture_ref, pressure_ref, gradient_ref, adjoint_ref, value_ref, total_ref,
):
    adjoint = relax(
        arrived_ref, row_hot_ref, col_hot_ref, weight_ref, count_ref, order_ref, parts_ref, start_ref, source_ref,
        value_ref, total_ref,
    )
    adjoint_ref[...] = adjoint
    pressure = pressure_ref[...]
    rows, cols = adjoint.shape
    row = lax.broadcasted_iota(jnp.int32, (rows, cols), 0) & (grid_size - 1)
    col = lax.broadcasted_iota(jnp.int32, (rows, cols), 1)
    inside = (row < grid_size - 1, row > 0, col < cols - 1, col > 0)
    total = jnp.zeros((rows, cols), jnp.float32)
    for keep, near_pressure, near_adjoint in zip(inside, shifted(pressure), shifted(adjoint), strict=True):
        total = total + jnp.where(keep, (pressure - near_pressure) * (adjoint - near_adjoint), 0.0)
    aperture = aperture_ref[...]
    gradient_ref[...] = -(aperture * aperture / 8.0) * total


def body(aperture, pressure, adj_source, trace_weight, end_device, end_local, trace_nodes):
    frac_count, grid_size, _ = aperture.shape
    owned_count, trace_len = trace_weight.shape
    device_count = lax.axis_size(AXES)
    rows, cols, width = frac_count * grid_size, grid_size, 2 * trace_len
    nodes = device_count * width
    per_block = math.gcd(device_count, 16)
    blocks = device_count // per_block
    in_vmem = pl.BlockSpec(memory_space=pltpu.VMEM)
    in_hbm = pl.BlockSpec(memory_space=pltpu.HBM)
    params = pltpu.CompilerParams(vmem_limit_bytes=(8 << 20) + nodes * 1024)
    landing = [
        pltpu.VMEM((blocks, per_block, 2 * width), jnp.bfloat16),
        pltpu.VMEM((rows, cols), jnp.float32),
    ]
    leaving = [
        pltpu.VMEM((2 * cols, rows), jnp.bfloat16),
        pltpu.VMEM((blocks, per_block, width), jnp.float32),
    ]

    def flat(field):
        return field.reshape(rows, cols)

    def vmem(*arrays):
        return [pltpu.with_memory_space_constraint(array, pltpu.VMEM) for array in arrays]

    def exchange(values):
        return lax.all_to_all(values, AXES, split_axis=0, concat_axis=0, tiled=True)

    field_shape = pltpu.VMEM((rows, cols), jnp.float32)
    arguments = (
        end_device.T, end_local.T, trace_nodes, trace_weight, flat(aperture), flat(adj_source), flat(pressure)
    )
    message, aperture_here, source_here, pressure_here = pl.pallas_call(
        functools.partial(pack_kernel, grid_size * grid_size),
        out_shape=[pltpu.VMEM((device_count, 4, width), jnp.float32)] + [field_shape] * 3,
        in_specs=[in_hbm] * 7,
        out_specs=[in_vmem] * 4,
        scratch_shapes=[
            pltpu.SMEM((2, owned_count), jnp.int32),
            pltpu.SMEM((2, owned_count), jnp.int32),
            pltpu.VMEM(trace_nodes.shape, jnp.int32),
            pltpu.VMEM(trace_weight.shape, jnp.float32),
            pltpu.SMEM((device_count,), jnp.int32),
            pltpu.SemaphoreType.DMA((4,)),
            pltpu.SemaphoreType.DMA((3,)),
        ],
        compiler_params=params,
        name="pack_ends",
    )(*[pltpu.with_memory_space_constraint(array, pltpu.HBM) for array in arguments])
    values_shape = pltpu.VMEM((device_count, 1, width), jnp.float32)
    values, row_hot, col_hot, col, weight, count, order, parts, adjoint = pl.pallas_call(
        functools.partial(first_kernel, grid_size),
        out_shape=[
            values_shape,
            pltpu.VMEM((blocks, rows, per_block * width), jnp.bfloat16),
            pltpu.VMEM((blocks, cols, per_block * width), jnp.bfloat16),
            pltpu.VMEM((blocks, per_block, width), jnp.int32),
            pltpu.VMEM((device_count, width), jnp.float32),
            pltpu.VMEM((device_count, width), jnp.int32),
            pltpu.VMEM((2, device_count, width), jnp.bfloat16),
            pltpu.VMEM((5, rows, cols), jnp.float32),
            field_shape,
        ],
        in_specs=[in_vmem] * 3,
        out_specs=[in_vmem] * 9,
        scratch_shapes=[pltpu.VMEM((blocks, per_block, width), jnp.bfloat16)] + landing + leaving,
        compiler_params=params,
        name="first_values",
    )(*vmem(exchange(message), aperture_here, source_here))
    for _ in range(SWEEPS - 1):
        values, adjoint = pl.pallas_call(
            sweep_kernel,
            out_shape=[values_shape, field_shape],
            in_specs=[in_vmem] * 10,
            out_specs=[in_vmem] * 2,
            scratch_shapes=landing + leaving,
            compiler_params=params,
            name="sweep",
        )(
            *vmem(
                exchange(values), row_hot, col_hot, col, weight, count, order, parts, adjoint, source_here
            )
        )
    gradient, adjoint = pl.pallas_call(
        functools.partial(last_kernel, grid_size),
        out_shape=[jax.ShapeDtypeStruct((rows, cols), jnp.float32)] * 2,
        in_specs=[in_vmem] * 11,
        out_specs=[in_vmem] * 2,
        scratch_shapes=landing,
        compiler_params=params,
        name="last_sweep",
    )(
        *vmem(
            exchange(values), row_hot, col_hot, weight, count, order, parts, adjoint,
            source_here, aperture_here, pressure_here,
        )
    )
    return gradient.reshape(aperture.shape), adjoint.reshape(aperture.shape)


def solution(mesh):
    fields, pairs = P(AXES, None, None), P(AXES, None)
    return jax.shard_map(
        body,
        mesh=mesh,
        in_specs=(fields, fields, fields, pairs, pairs, pairs, fields),
        out_specs=(fields, fields),
        check_vma=False,
    )
```

```python
import functools
import math

import jax
import jax.numpy as jnp
from jax import lax
from jax.experimental import pallas as pl
from jax.experimental.pallas import tpu as pltpu
from jax.sharding import PartitionSpec as P

SWEEPS = 3
INNER = 8
LEAKAGE = 0.25
AXES = ("wide", "narrow")
SLICE = 8


def pack_kernel(
    cells_per, dest_hbm, local_hbm, nodes_hbm, weight_hbm, aperture_hbm, source_hbm, pressure_hbm,
    out_ref, aperture_ref, source_ref, pressure_ref,
    dest_ref, local_ref, nodes_ref, weight_ref, seen_ref, small_sems, large_sems,
):
    owned = nodes_ref.shape[0]
    devices, _, width = out_ref.shape
    small = [
        pltpu.make_async_copy(source, target, small_sems.at[index])
        for index, (source, target) in enumerate(
            ((dest_hbm, dest_ref), (local_hbm, local_ref), (nodes_hbm, nodes_ref), (weight_hbm, weight_ref))
        )
    ]
    large = [
        pltpu.make_async_copy(source, target, large_sems.at[index])
        for index, (source, target) in enumerate(
            ((aperture_hbm, aperture_ref), (source_hbm, source_ref), (pressure_hbm, pressure_ref))
        )
    ]
    for copy in small + large:
        copy.start()

    def clear(device, carry):
        seen_ref[device] = 0
        return carry

    lax.fori_loop(0, devices, clear, 0, unroll=8)
    out_ref[:, 0:2, :] = jnp.zeros((devices, 2, width), jnp.float32)
    out_ref[:, 2:4, :] = jnp.full((devices, 2, width), -1.0, jnp.float32)
    for copy in small:
        copy.wait()

    def place(index, carry):
        ends = [dest_ref[0, index], dest_ref[1, index]]
        weights = weight_ref[pl.ds(index, 1), :]
        for side in range(2):
            target = ends[side]
            rank = seen_ref[target]
            seen_ref[target] = rank + 1
            first = local_ref[side, index] * cells_per + 1
            cells = (nodes_ref[index, side : side + 1, :] + first).astype(jnp.float32)
            out_ref[target, pl.ds(rank, 1), :] = jnp.concatenate([cells, weights], axis=1)
            out_ref[target, pl.ds(rank + 2, 1), :] = jnp.full(
                (1, width), ends[1 - side].astype(jnp.float32)
            )
        return carry

    lax.fori_loop(0, owned, place, 0, unroll=True)
    for copy in large:
        copy.wait()


def face_parts(conduct, grid_size):
    rows, cols = conduct.shape
    row = lax.broadcasted_iota(jnp.int32, (rows, cols), 0) & (grid_size - 1)
    col = lax.broadcasted_iota(jnp.int32, (rows, cols), 1)
    below = jnp.where(row < grid_size - 1, (conduct + pltpu.roll(conduct, rows - 1, 0)) * 0.5, 0.0)
    above = jnp.where(row > 0, (conduct + pltpu.roll(conduct, 1, 0)) * 0.5, 0.0)
    right = jnp.where(col < cols - 1, (conduct + pltpu.roll(conduct, cols - 1, 1)) * 0.5, 0.0)
    left = jnp.where(col > 0, (conduct + pltpu.roll(conduct, 1, 1)) * 0.5, 0.0)
    return below, above, right, left


def split_pair(values):
    high_part = values.astype(jnp.bfloat16)
    low_part = (values - high_part.astype(jnp.float32)).astype(jnp.bfloat16)
    return high_part, low_part


def split_three(values):
    high_part, low_part = split_pair(values)
    rest = values - high_part.astype(jnp.float32) - low_part.astype(jnp.float32)
    return high_part, low_part, rest.astype(jnp.bfloat16)


def over_blocks(count_ref, blocks, work):
    per_block = count_ref.shape[0] // blocks
    work(0)
    if blocks > 1:
        needed = lax.div(count_ref[0, 0] + (per_block - 1), per_block)

        def step(block, carry):
            work(block)
            return carry

        lax.fori_loop(1, needed, step, 0)


def spread(row_hot_ref, col_hot_ref, total_ref, value_of, block):
    _, cols, lanes = col_hot_ref.shape
    group = 2
    width = value_of(block, 0).shape[1]
    total = None
    for start in range(0, lanes // width, group):
        parts = [[], []]
        for device in range(start, start + group):
            hot = col_hot_ref[block, :, device * width : (device + 1) * width]
            for part, value in zip(parts, split_pair(value_of(block, device)), strict=True):
                part.append(hot * value)
        right = jnp.concatenate([jnp.concatenate(part, axis=1) for part in parts], axis=0)
        product = lax.dot_general(
            row_hot_ref[block, :, start * width : (start + group) * width],
            right,
            (((1,), (1,)), ((), ())),
            preferred_element_type=jnp.float32,
        )
        total = product if total is None else total + product
    total = total[:, :cols] + total[:, cols:]
    if isinstance(block, int):
        total_ref[...] = total
    else:
        total_ref[...] += total


def gather(row_hot_ref, col_ref, peer_ref, both_ref, values_ref, block):
    _, per_block, width = col_ref.shape
    cols = both_ref.shape[0] // 2
    group = 2
    col_ids = lax.broadcasted_iota(jnp.int32, (cols, width), 0)
    both = both_ref[...]
    for start in range(0, per_block, group):
        picked = jnp.dot(
            both,
            row_hot_ref[block, :, start * width : (start + group) * width],
            preferred_element_type=jnp.float32,
        )
        picked = picked[:cols] + picked[cols:]
        for offset in range(group):
            device = start + offset
            mine = picked[:, offset * width : (offset + 1) * width]
            hit = col_ids == col_ref[block, device : device + 1, :]
            values_ref[peer_ref[block, device, 0]] = jnp.sum(
                jnp.where(hit, mine, 0.0), axis=0, keepdims=True
            )


def send_values(adjoint, row_hot_ref, col_ref, count_ref, peer_ref, both_ref, values_ref):
    values_ref[...] = jnp.zeros(values_ref.shape, jnp.float32)
    both_ref[...] = jnp.concatenate(split_pair(adjoint.T), axis=0)
    over_blocks(
        count_ref, col_ref.shape[0],
        lambda block: gather(row_hot_ref, col_ref, peer_ref, both_ref, values_ref, block),
    )


def first_kernel(
    grid_size, message_ref, aperture_ref, source_ref,
    values_ref, row_hot_ref, col_hot_ref, col_ref, weight_ref, count_ref, peer_ref, parts_ref, adjoint_ref,
    row_ref, total_ref, both_ref,
):
    devices, _, width = message_ref.shape
    trace_len = width // 2
    blocks, per_block, _ = col_ref.shape
    rows, cols = aperture_ref.shape
    slots = [message_ref[:, rank, :] for rank in range(2)]
    partners = [message_ref[:, 2 + rank, :] for rank in range(2)]
    down = lax.broadcasted_iota(jnp.int32, (devices, width), 0)
    along = lax.broadcasted_iota(jnp.int32, (devices, width), 1)
    device_id = down.astype(jnp.float32)
    target = [
        jnp.sum(jnp.where(down == along, partners[rank], 0.0), axis=0, keepdims=True) for rank in range(2)
    ]
    target = [jnp.where(along[0:1] < devices, target[rank], -1.0) for rank in range(2)]
    used = jnp.where((device_id == target[0]) | (device_id == target[1]), 1.0, 0.0)
    used = jnp.max(used, axis=1, keepdims=True)
    count = jnp.sum(used, axis=0, keepdims=True)
    packed = jnp.zeros((2 * devices, 4 * width), jnp.float32)
    for rank in range(2):
        place = jnp.sum(jnp.where(device_id < target[rank], used, 0.0), axis=0, keepdims=True)
        ahead = (down < along) if rank == 0 else (down <= along)
        earlier = jnp.where((partners[0] == target[rank]) & ahead, 1.0, 0.0)
        earlier = earlier + jnp.where((partners[1] == target[rank]) & (down < along), 1.0, 0.0)
        spot = jnp.sum(earlier, axis=0, keepdims=True)
        here = (device_id == place) & (target[rank] >= 0.0)
        pick = [jnp.where(here & (spot == float(index)), 1.0, 0.0).astype(jnp.bfloat16) for index in range(2)]
        packed = packed + jnp.dot(
            jnp.concatenate(pick, axis=0)[:, :devices],
            jnp.concatenate(split_three(slots[rank]) + (partners[rank].astype(jnp.bfloat16),), axis=1),
            preferred_element_type=jnp.float32,
        )
    ends = packed[:, :width] + packed[:, width : 2 * width] + packed[:, 2 * width : 3 * width]
    ends = [ends[:devices], ends[devices:]]
    front = along < trace_len
    cell = jnp.where(front, ends[0], pltpu.roll(ends[1], trace_len, 1)).astype(jnp.int32) - 1
    weight = jnp.where(front, pltpu.roll(ends[0], trace_len, 1), ends[1])
    me = lax.axis_index(AXES)
    peer = jnp.where(device_id < count, packed[:devices, 3 * width :].astype(jnp.int32), me)
    count_ref[...] = jnp.broadcast_to(count, count_ref.shape).astype(jnp.int32)
    peer_ref[...] = peer.reshape(peer_ref.shape)
    weight_ref[...] = weight.reshape(weight_ref.shape)
    row_ref[...] = (cell >> (grid_size.bit_length() - 1)).reshape(row_ref.shape)
    col_ref[...] = (cell & (grid_size - 1)).reshape(col_ref.shape)
    cell_ids = lax.broadcasted_iota(jnp.int32, (rows, width), 0).astype(jnp.float32).astype(jnp.bfloat16)
    one, zero = jnp.ones((), jnp.bfloat16), jnp.zeros((), jnp.bfloat16)

    def build(block):
        block_cols = col_ref[block].astype(jnp.float32).astype(jnp.bfloat16)
        block_rows = row_ref[block].astype(jnp.float32).astype(jnp.bfloat16)
        for device in range(per_block):
            lanes = slice(device * width, (device + 1) * width)
            row_hot_ref[block, :, lanes] = jnp.where(cell_ids == block_rows[device : device + 1], one, zero)
            col_hot_ref[block, :, lanes] = jnp.where(
                cell_ids[:cols] == block_cols[device : device + 1], one, zero
            )
        spread(
            row_hot_ref, col_hot_ref, total_ref,
            lambda block, device: weight_ref[block, device : device + 1, :], block,
        )

    over_blocks(count_ref, blocks, build)
    aperture = aperture_ref[...]
    faces = face_parts(aperture * aperture * aperture / 12.0, grid_size)
    inv_diag = 1.0 / (LEAKAGE + (faces[0] + faces[1] + faces[2] + faces[3]) + total_ref[...])
    for index in range(4):
        parts_ref[index] = faces[index] * inv_diag
    parts_ref[4] = inv_diag
    adjoint = source_ref[...] * inv_diag
    adjoint_ref[...] = adjoint
    send_values(adjoint, row_hot_ref, col_ref, count_ref, peer_ref, both_ref, values_ref)


def near(state_ref, rows):
    cols = state_ref.shape[1]
    first = SLICE + rows
    here = state_ref[first : first + SLICE]
    return here, (
        state_ref[first + 1 : first + SLICE + 1],
        state_ref[first - 1 : first + SLICE - 1],
        pltpu.roll(here, cols - 1, 1),
        pltpu.roll(here, 1, 1),
    )


def relax(
    arrived_ref, row_hot_ref, col_hot_ref, weight_ref, count_ref, peer_ref, parts_ref, start_ref, source_ref,
    adjoint_ref, total_ref, early_ref, state_ref, before_ref=None,
):
    rows, cols = start_ref.shape
    slices = range(0, rows, SLICE)
    margin = jnp.zeros((SLICE, cols), jnp.float32)
    for index in range(2):
        state_ref[index, 0:SLICE] = margin
        state_ref[index, SLICE + rows :] = margin
    state_ref[0, SLICE : SLICE + rows] = start_ref[...]

    def pull(state, first):
        _, (below, above, right, left) = near(state, first)
        here = slice(first, first + SLICE)
        return (parts_ref[0, here] * below + parts_ref[1, here] * above) + (
            parts_ref[2, here] * right + parts_ref[3, here] * left
        )

    for first in slices:
        early_ref[first : first + SLICE] = pull(state_ref.at[0], first)
    if before_ref is not None:
        before_ref()
    over_blocks(
        count_ref, weight_ref.shape[0],
        lambda block: spread(
            row_hot_ref, col_hot_ref, total_ref,
            lambda block, device: weight_ref[block, device : device + 1, :] * arrived_ref[peer_ref[block, device, 0]],
            block,
        ),
    )
    for step in range(INNER):
        old, new = state_ref.at[step % 2], state_ref.at[(step + 1) % 2]
        for first in slices:
            here = slice(first, first + SLICE)
            if step == 0:
                forcing = (source_ref[here] + total_ref[here]) * parts_ref[4, here]
                total_ref[here] = forcing
                now = forcing + early_ref[here]
            else:
                now = total_ref[here] + pull(old, first)
            new[SLICE + first : 2 * SLICE + first] = now
            if step == INNER - 1:
                adjoint_ref[here] = now


def sweep_kernel(
    arrived_ref, row_hot_ref, col_hot_ref, col_ref, weight_ref, count_ref, peer_ref, parts_ref, start_ref,
    source_ref, values_ref, adjoint_ref, total_ref, early_ref, state_ref, both_ref,
):
    relax(
        arrived_ref, row_hot_ref, col_hot_ref, weight_ref, count_ref, peer_ref, parts_ref, start_ref, source_ref,
        adjoint_ref, total_ref, early_ref, state_ref,
    )
    send_values(adjoint_ref[...], row_hot_ref, col_ref, count_ref, peer_ref, both_ref, values_ref)


def last_kernel(
    grid_size, arrived_ref, row_hot_ref, col_hot_ref, weight_ref, count_ref, peer_ref, parts_ref, start_ref,
    source_ref, aperture_ref, pressure_ref, gradient_hbm, adjoint_hbm,
    total_ref, early_ref, state_ref, share_ref, gradient_ref, adjoint_ref, sems,
):
    rows, cols = start_ref.shape
    slices = range(0, rows, SLICE)

    def shares():
        aperture = aperture_ref[...]
        scale = -(aperture * aperture / 8.0)
        pressure = pressure_ref[...]
        row = lax.broadcasted_iota(jnp.int32, (rows, cols), 0) & (grid_size - 1)
        col = lax.broadcasted_iota(jnp.int32, (rows, cols), 1)
        inside = (row < grid_size - 1, row > 0, col < cols - 1, col > 0)
        turns = ((rows - 1, 0), (1, 0), (cols - 1, 1), (1, 1))
        for index in range(4):
            share_ref[index] = jnp.where(
                inside[index], scale * (pressure - pltpu.roll(pressure, *turns[index])), 0.0
            )

    relax(
        arrived_ref, row_hot_ref, col_hot_ref, weight_ref, count_ref, peer_ref, parts_ref, start_ref, source_ref,
        adjoint_ref, total_ref, early_ref, state_ref, shares,
    )
    keep = pltpu.make_async_copy(adjoint_ref, adjoint_hbm, sems.at[0])
    keep.start()
    last_state = state_ref.at[INNER % 2]
    for first in slices:
        here, sides = near(last_state, first)
        lines = slice(first, first + SLICE)
        terms = [share_ref[index, lines] * (here - side) for index, side in enumerate(sides)]
        gradient_ref[lines] = (terms[0] + terms[1]) + (terms[2] + terms[3])
    send = pltpu.make_async_copy(gradient_ref, gradient_hbm, sems.at[1])
    send.start()
    keep.wait()
    send.wait()


def body(aperture, pressure, adj_source, trace_weight, end_device, end_local, trace_nodes):
    frac_count, grid_size, _ = aperture.shape
    owned_count, trace_len = trace_weight.shape
    device_count = lax.axis_size(AXES)
    rows, cols, width = frac_count * grid_size, grid_size, 2 * trace_len
    nodes = device_count * width
    per_block = math.gcd(device_count, 16)
    blocks = device_count // per_block
    in_vmem = pl.BlockSpec(memory_space=pltpu.VMEM)
    in_hbm = pl.BlockSpec(memory_space=pltpu.HBM)
    params = pltpu.CompilerParams(vmem_limit_bytes=(8 << 20) + nodes * 1024)
    field = pltpu.VMEM((rows, cols), jnp.float32)
    sweeping = [field, field, pltpu.VMEM((2, rows + 2 * SLICE, cols), jnp.float32)]
    leaving = [pltpu.VMEM((2 * cols, rows), jnp.bfloat16)]
    ends_int = pltpu.VMEM((blocks, per_block, width), jnp.int32)
    ends_float = pltpu.VMEM((blocks, per_block, width), jnp.float32)

    def flat(whole):
        return whole.reshape(rows, cols)

    def vmem(*arrays):
        return [pltpu.with_memory_space_constraint(array, pltpu.VMEM) for array in arrays]

    def exchange(values):
        return lax.all_to_all(values, AXES, split_axis=0, concat_axis=0, tiled=True)

    arguments = (
        end_device.T, end_local.T, trace_nodes, trace_weight, flat(aperture), flat(adj_source), flat(pressure)
    )
    message, aperture_here, source_here, pressure_here = pl.pallas_call(
        functools.partial(pack_kernel, grid_size * grid_size),
        out_shape=[pltpu.VMEM((device_count, 4, width), jnp.float32)] + [field] * 3,
        in_specs=[in_hbm] * 7,
        out_specs=[in_vmem] * 4,
        scratch_shapes=[
            pltpu.SMEM((2, owned_count), jnp.int32),
            pltpu.SMEM((2, owned_count), jnp.int32),
            pltpu.VMEM(trace_nodes.shape, jnp.int32),
            pltpu.VMEM(trace_weight.shape, jnp.float32),
            pltpu.SMEM((device_count,), jnp.int32),
            pltpu.SemaphoreType.DMA((4,)),
            pltpu.SemaphoreType.DMA((3,)),
        ],
        compiler_params=params,
        name="pack_ends",
    )(*[pltpu.with_memory_space_constraint(array, pltpu.HBM) for array in arguments])
    values_shape = pltpu.VMEM((device_count, 1, width), jnp.float32)
    values, row_hot, col_hot, col, weight, count, peer, parts, adjoint = pl.pallas_call(
        functools.partial(first_kernel, grid_size),
        out_shape=[
            values_shape,
            pltpu.VMEM((blocks, rows, per_block * width), jnp.bfloat16),
            pltpu.VMEM((blocks, cols, per_block * width), jnp.bfloat16),
            ends_int,
            ends_float,
            pltpu.VMEM((device_count, width), jnp.int32),
            ends_int,
            pltpu.VMEM((5, rows, cols), jnp.float32),
            field,
        ],
        in_specs=[in_vmem] * 3,
        out_specs=[in_vmem] * 9,
        scratch_shapes=[ends_int, field] + leaving,
        compiler_params=params,
        name="first_values",
    )(*vmem(exchange(message), aperture_here, source_here))
    for _ in range(SWEEPS - 1):
        values, adjoint = pl.pallas_call(
            sweep_kernel,
            out_shape=[values_shape, field],
            in_specs=[in_vmem] * 10,
            out_specs=[in_vmem] * 2,
            scratch_shapes=sweeping + leaving,
            compiler_params=params,
            name="sweep",
        )(
            *vmem(
                exchange(values), row_hot, col_hot, col, weight, count, peer, parts, adjoint, source_here
            )
        )
    gradient, adjoint = pl.pallas_call(
        functools.partial(last_kernel, grid_size),
        out_shape=[jax.ShapeDtypeStruct((rows, cols), jnp.float32)] * 2,
        in_specs=[in_vmem] * 11,
        out_specs=[in_hbm] * 2,
        scratch_shapes=sweeping
        + [pltpu.VMEM((4, rows, cols), jnp.float32), field, field, pltpu.SemaphoreType.DMA((2,))],
        compiler_params=params,
        name="last_sweep",
    )(
        *vmem(
            exchange(values), row_hot, col_hot, weight, count, peer, parts, adjoint,
            source_here, aperture_here, pressure_here,
        )
    )
    return gradient.reshape(aperture.shape), adjoint.reshape(aperture.shape)


def solution(mesh):
    fields, pairs = P(AXES, None, None), P(AXES, None)
    return jax.shard_map(
        body,
        mesh=mesh,
        in_specs=(fields, fields, fields, pairs, pairs, pairs, fields),
        out_specs=(fields, fields),
        check_vma=False,
    )
```

```python
import functools
import math

import jax
import jax.numpy as jnp
from jax import lax
from jax.experimental import pallas as pl
from jax.experimental.pallas import tpu as pltpu
from jax.sharding import PartitionSpec as P

SWEEPS = 3
INNER = 8
LEAKAGE = 0.25
AXES = ("wide", "narrow")
SLICE = 8


def start_copies(pairs, sems):
    copies = [
        pltpu.make_async_copy(source, target, sems.at[index]) for index, (source, target) in enumerate(pairs)
    ]
    for copy in copies:
        copy.start()
    return copies


def pack_kernel(
    cells_per, dest_hbm, local_hbm, nodes_hbm, weight_hbm, aperture_hbm,
    out_ref, aperture_ref, dest_ref, local_ref, nodes_ref, weight_ref, seen_ref, sems,
):
    owned = nodes_ref.shape[0]
    devices, _, width = out_ref.shape
    copies = start_copies(
        (
            (dest_hbm, dest_ref), (local_hbm, local_ref), (nodes_hbm, nodes_ref), (weight_hbm, weight_ref),
            (aperture_hbm, aperture_ref),
        ),
        sems,
    )

    def clear(device, carry):
        seen_ref[device] = 0
        return carry

    lax.fori_loop(0, devices, clear, 0, unroll=8)
    out_ref[:, 0:2, :] = jnp.zeros((devices, 2, width), jnp.float32)
    out_ref[:, 2:4, :] = jnp.full((devices, 2, width), -1.0, jnp.float32)
    for copy in copies[:4]:
        copy.wait()

    def place(index, carry):
        ends = [dest_ref[0, index], dest_ref[1, index]]
        weights = weight_ref[pl.ds(index, 1), :]
        for side in range(2):
            target = ends[side]
            rank = seen_ref[target]
            seen_ref[target] = rank + 1
            first = local_ref[side, index] * cells_per + 1
            cells = (nodes_ref[index, side : side + 1, :] + first).astype(jnp.float32)
            out_ref[target, pl.ds(rank, 1), :] = jnp.concatenate([cells, weights], axis=1)
            out_ref[target, pl.ds(rank + 2, 1), :] = jnp.full(
                (1, width), ends[1 - side].astype(jnp.float32)
            )
        return carry

    lax.fori_loop(0, owned, place, 0, unroll=True)
    copies[4].wait()


def face_parts(conduct, grid_size):
    rows, cols = conduct.shape
    row = lax.broadcasted_iota(jnp.int32, (rows, cols), 0) & (grid_size - 1)
    col = lax.broadcasted_iota(jnp.int32, (rows, cols), 1)
    below = jnp.where(row < grid_size - 1, (conduct + pltpu.roll(conduct, rows - 1, 0)) * 0.5, 0.0)
    above = jnp.where(row > 0, (conduct + pltpu.roll(conduct, 1, 0)) * 0.5, 0.0)
    right = jnp.where(col < cols - 1, (conduct + pltpu.roll(conduct, cols - 1, 1)) * 0.5, 0.0)
    left = jnp.where(col > 0, (conduct + pltpu.roll(conduct, 1, 1)) * 0.5, 0.0)
    return below, above, right, left


def split_pair(values):
    high_part = values.astype(jnp.bfloat16)
    low_part = (values - high_part.astype(jnp.float32)).astype(jnp.bfloat16)
    return high_part, low_part


def split_three(values):
    high_part, low_part = split_pair(values)
    rest = values - high_part.astype(jnp.float32) - low_part.astype(jnp.float32)
    return high_part, low_part, rest.astype(jnp.bfloat16)


def over_blocks(count_ref, blocks, work):
    per_block = count_ref.shape[0] // blocks
    work(0)
    if blocks > 1:
        needed = lax.div(count_ref[0, 0] + (per_block - 1), per_block)

        def step(block, carry):
            work(block)
            return carry

        lax.fori_loop(1, needed, step, 0)


def spread(row_hot_ref, col_hot_ref, total_ref, value_of, block):
    _, cols, lanes = col_hot_ref.shape
    group = 2
    width = value_of(block, 0).shape[1]
    total = None
    for start in range(0, lanes // width, group):
        parts = [[], []]
        for device in range(start, start + group):
            hot = col_hot_ref[block, :, device * width : (device + 1) * width]
            for part, value in zip(parts, split_pair(value_of(block, device)), strict=True):
                part.append(hot * value)
        right = jnp.concatenate([jnp.concatenate(part, axis=1) for part in parts], axis=0)
        product = lax.dot_general(
            row_hot_ref[block, :, start * width : (start + group) * width],
            right,
            (((1,), (1,)), ((), ())),
            preferred_element_type=jnp.float32,
        )
        total = product if total is None else total + product
    total = total[:, :cols] + total[:, cols:]
    if isinstance(block, int):
        total_ref[...] = total
    else:
        total_ref[...] += total


def gather(row_hot_ref, col_ref, peer_ref, both_ref, values_ref, block):
    _, per_block, width = col_ref.shape
    cols = both_ref.shape[0] // 2
    group = 2
    col_ids = lax.broadcasted_iota(jnp.int32, (cols, width), 0)
    both = both_ref[...]
    for start in range(0, per_block, group):
        picked = jnp.dot(
            both,
            row_hot_ref[block, :, start * width : (start + group) * width],
            preferred_element_type=jnp.float32,
        )
        picked = picked[:cols] + picked[cols:]
        for offset in range(group):
            device = start + offset
            mine = picked[:, offset * width : (offset + 1) * width]
            hit = col_ids == col_ref[block, device : device + 1, :]
            values_ref[peer_ref[block, device, 0]] = jnp.sum(
                jnp.where(hit, mine, 0.0), axis=0, keepdims=True
            )


def send_values(adjoint, row_hot_ref, col_ref, count_ref, peer_ref, both_ref, values_ref):
    values_ref[...] = jnp.zeros(values_ref.shape, jnp.float32)
    both_ref[...] = jnp.concatenate(split_pair(adjoint.T), axis=0)
    over_blocks(
        count_ref, col_ref.shape[0],
        lambda block: gather(row_hot_ref, col_ref, peer_ref, both_ref, values_ref, block),
    )


def first_kernel(
    grid_size, message_ref, aperture_ref, source_hbm, pressure_hbm,
    values_ref, row_hot_ref, col_hot_ref, col_ref, weight_ref, count_ref, peer_ref, parts_ref, adjoint_ref,
    source_ref, pressure_ref, row_ref, total_ref, both_ref, sems,
):
    copies = start_copies(
        ((source_hbm, source_ref), (pressure_hbm, pressure_ref)), sems
    )
    devices, _, width = message_ref.shape
    trace_len = width // 2
    blocks, per_block, _ = col_ref.shape
    rows, cols = aperture_ref.shape
    aperture = aperture_ref[...]
    faces = face_parts(aperture * aperture * aperture / 12.0, grid_size)
    for index in range(4):
        parts_ref[index] = faces[index]
    parts_ref[4] = LEAKAGE + (faces[0] + faces[1] + faces[2] + faces[3])
    slots = [message_ref[:, rank, :] for rank in range(2)]
    partners = [message_ref[:, 2 + rank, :] for rank in range(2)]
    down = lax.broadcasted_iota(jnp.int32, (devices, width), 0)
    along = lax.broadcasted_iota(jnp.int32, (devices, width), 1)
    device_id = down.astype(jnp.float32)
    target = [
        jnp.sum(jnp.where(down == along, partners[rank], 0.0), axis=0, keepdims=True) for rank in range(2)
    ]
    target = [jnp.where(along[0:1] < devices, target[rank], -1.0) for rank in range(2)]
    used = jnp.where((device_id == target[0]) | (device_id == target[1]), 1.0, 0.0)
    used = jnp.max(used, axis=1, keepdims=True)
    count = jnp.sum(used, axis=0, keepdims=True)
    packed = jnp.zeros((2 * devices, 4 * width), jnp.float32)
    for rank in range(2):
        place = jnp.sum(jnp.where(device_id < target[rank], used, 0.0), axis=0, keepdims=True)
        ahead = (down < along) if rank == 0 else (down <= along)
        earlier = jnp.where((partners[0] == target[rank]) & ahead, 1.0, 0.0)
        earlier = earlier + jnp.where((partners[1] == target[rank]) & (down < along), 1.0, 0.0)
        spot = jnp.sum(earlier, axis=0, keepdims=True)
        here = (device_id == place) & (target[rank] >= 0.0)
        pick = [jnp.where(here & (spot == float(index)), 1.0, 0.0).astype(jnp.bfloat16) for index in range(2)]
        packed = packed + jnp.dot(
            jnp.concatenate(pick, axis=0)[:, :devices],
            jnp.concatenate(split_three(slots[rank]) + (partners[rank].astype(jnp.bfloat16),), axis=1),
            preferred_element_type=jnp.float32,
        )
    ends = packed[:, :width] + packed[:, width : 2 * width] + packed[:, 2 * width : 3 * width]
    ends = [ends[:devices], ends[devices:]]
    front = along < trace_len
    cell = jnp.where(front, ends[0], pltpu.roll(ends[1], trace_len, 1)).astype(jnp.int32) - 1
    weight = jnp.where(front, pltpu.roll(ends[0], trace_len, 1), ends[1])
    me = lax.axis_index(AXES)
    peer = jnp.where(device_id < count, packed[:devices, 3 * width :].astype(jnp.int32), me)
    count_ref[...] = jnp.broadcast_to(count, count_ref.shape).astype(jnp.int32)
    peer_ref[...] = peer.reshape(peer_ref.shape)
    weight_ref[...] = weight.reshape(weight_ref.shape)
    row_ref[...] = (cell >> (grid_size.bit_length() - 1)).reshape(row_ref.shape)
    col_ref[...] = (cell & (grid_size - 1)).reshape(col_ref.shape)
    cell_ids = lax.broadcasted_iota(jnp.int32, (rows, width), 0).astype(jnp.float32).astype(jnp.bfloat16)
    one, zero = jnp.ones((), jnp.bfloat16), jnp.zeros((), jnp.bfloat16)

    def build(block):
        block_cols = col_ref[block].astype(jnp.float32).astype(jnp.bfloat16)
        block_rows = row_ref[block].astype(jnp.float32).astype(jnp.bfloat16)
        for device in range(per_block):
            lanes = slice(device * width, (device + 1) * width)
            row_hot_ref[block, :, lanes] = jnp.where(cell_ids == block_rows[device : device + 1], one, zero)
            col_hot_ref[block, :, lanes] = jnp.where(
                cell_ids[:cols] == block_cols[device : device + 1], one, zero
            )
        spread(
            row_hot_ref, col_hot_ref, total_ref,
            lambda block, device: weight_ref[block, device : device + 1, :], block,
        )

    over_blocks(count_ref, blocks, build)
    inv_diag = 1.0 / (parts_ref[4] + total_ref[...])
    for copy in copies:
        copy.wait()
    for index in range(4):
        parts_ref[index] = parts_ref[index] * inv_diag
    parts_ref[4] = inv_diag
    adjoint = source_ref[...] * inv_diag
    adjoint_ref[...] = adjoint
    send_values(adjoint, row_hot_ref, col_ref, count_ref, peer_ref, both_ref, values_ref)


def near(state_ref, rows):
    cols = state_ref.shape[1]
    first = SLICE + rows
    here = state_ref[first : first + SLICE]
    return here, (
        state_ref[first + 1 : first + SLICE + 1],
        state_ref[first - 1 : first + SLICE - 1],
        pltpu.roll(here, cols - 1, 1),
        pltpu.roll(here, 1, 1),
    )


def relax(
    arrived_ref, row_hot_ref, col_hot_ref, weight_ref, count_ref, peer_ref, parts_ref, start_ref, source_ref,
    adjoint_ref, total_ref, early_ref, state_ref, before_ref=None,
):
    rows, cols = start_ref.shape
    slices = range(0, rows, SLICE)
    margin = jnp.zeros((SLICE, cols), jnp.float32)
    for index in range(2):
        state_ref[index, 0:SLICE] = margin
        state_ref[index, SLICE + rows :] = margin
    state_ref[0, SLICE : SLICE + rows] = start_ref[...]

    def pull(state, first):
        _, (below, above, right, left) = near(state, first)
        here = slice(first, first + SLICE)
        return (parts_ref[0, here] * below + parts_ref[1, here] * above) + (
            parts_ref[2, here] * right + parts_ref[3, here] * left
        )

    for first in slices:
        early_ref[first : first + SLICE] = pull(state_ref.at[0], first)
    if before_ref is not None:
        before_ref()
    over_blocks(
        count_ref, weight_ref.shape[0],
        lambda block: spread(
            row_hot_ref, col_hot_ref, total_ref,
            lambda block, device: weight_ref[block, device : device + 1, :] * arrived_ref[peer_ref[block, device, 0]],
            block,
        ),
    )
    for step in range(INNER):
        old, new = state_ref.at[step % 2], state_ref.at[(step + 1) % 2]
        for first in slices:
            here = slice(first, first + SLICE)
            if step == 0:
                forcing = (source_ref[here] + total_ref[here]) * parts_ref[4, here]
                total_ref[here] = forcing
                now = forcing + early_ref[here]
            else:
                now = total_ref[here] + pull(old, first)
            new[SLICE + first : 2 * SLICE + first] = now
            if step == INNER - 1:
                adjoint_ref[here] = now


def sweep_kernel(
    arrived_ref, row_hot_ref, col_hot_ref, col_ref, weight_ref, count_ref, peer_ref, parts_ref, start_ref,
    source_ref, values_ref, adjoint_ref, total_ref, early_ref, state_ref, both_ref,
):
    relax(
        arrived_ref, row_hot_ref, col_hot_ref, weight_ref, count_ref, peer_ref, parts_ref, start_ref, source_ref,
        adjoint_ref, total_ref, early_ref, state_ref,
    )
    send_values(adjoint_ref[...], row_hot_ref, col_ref, count_ref, peer_ref, both_ref, values_ref)


def last_kernel(
    grid_size, arrived_ref, row_hot_ref, col_hot_ref, weight_ref, count_ref, peer_ref, parts_ref, start_ref,
    source_ref, aperture_ref, pressure_ref, gradient_hbm, adjoint_hbm,
    total_ref, early_ref, state_ref, share_ref, gradient_ref, adjoint_ref, sems,
):
    rows, cols = start_ref.shape
    slices = range(0, rows, SLICE)

    def shares():
        aperture = aperture_ref[...]
        scale = -(aperture * aperture / 8.0)
        pressure = pressure_ref[...]
        row = lax.broadcasted_iota(jnp.int32, (rows, cols), 0) & (grid_size - 1)
        col = lax.broadcasted_iota(jnp.int32, (rows, cols), 1)
        inside = (row < grid_size - 1, row > 0, col < cols - 1, col > 0)
        turns = ((rows - 1, 0), (1, 0), (cols - 1, 1), (1, 1))
        for index in range(4):
            share_ref[index] = jnp.where(
                inside[index], scale * (pressure - pltpu.roll(pressure, *turns[index])), 0.0
            )

    relax(
        arrived_ref, row_hot_ref, col_hot_ref, weight_ref, count_ref, peer_ref, parts_ref, start_ref, source_ref,
        adjoint_ref, total_ref, early_ref, state_ref, shares,
    )
    keep = pltpu.make_async_copy(adjoint_ref, adjoint_hbm, sems.at[0])
    keep.start()
    last_state = state_ref.at[INNER % 2]
    for first in slices:
        here, sides = near(last_state, first)
        lines = slice(first, first + SLICE)
        terms = [share_ref[index, lines] * (here - side) for index, side in enumerate(sides)]
        gradient_ref[lines] = (terms[0] + terms[1]) + (terms[2] + terms[3])
    send = pltpu.make_async_copy(gradient_ref, gradient_hbm, sems.at[1])
    send.start()
    keep.wait()
    send.wait()


def body(aperture, pressure, adj_source, trace_weight, end_device, end_local, trace_nodes):
    frac_count, grid_size, _ = aperture.shape
    owned_count, trace_len = trace_weight.shape
    device_count = lax.axis_size(AXES)
    rows, cols, width = frac_count * grid_size, grid_size, 2 * trace_len
    nodes = device_count * width
    per_block = math.gcd(device_count, 16)
    blocks = device_count // per_block
    in_vmem = pl.BlockSpec(memory_space=pltpu.VMEM)
    in_hbm = pl.BlockSpec(memory_space=pltpu.HBM)
    params = pltpu.CompilerParams(vmem_limit_bytes=(8 << 20) + nodes * 1024)
    field = pltpu.VMEM((rows, cols), jnp.float32)
    sweeping = [field, field, pltpu.VMEM((2, rows + 2 * SLICE, cols), jnp.float32)]
    leaving = [pltpu.VMEM((2 * cols, rows), jnp.bfloat16)]
    ends_int = pltpu.VMEM((blocks, per_block, width), jnp.int32)
    ends_float = pltpu.VMEM((blocks, per_block, width), jnp.float32)

    def flat(whole):
        return whole.reshape(rows, cols)

    def vmem(*arrays):
        return [pltpu.with_memory_space_constraint(array, pltpu.VMEM) for array in arrays]

    def hbm(*arrays):
        return [pltpu.with_memory_space_constraint(array, pltpu.HBM) for array in arrays]

    def exchange(values):
        return lax.all_to_all(values, AXES, split_axis=0, concat_axis=0, tiled=True)

    message, aperture_here = pl.pallas_call(
        functools.partial(pack_kernel, grid_size * grid_size),
        out_shape=[pltpu.VMEM((device_count, 4, width), jnp.float32), field],
        in_specs=[in_hbm] * 5,
        out_specs=[in_vmem] * 2,
        scratch_shapes=[
            pltpu.SMEM((2, owned_count), jnp.int32),
            pltpu.SMEM((2, owned_count), jnp.int32),
            pltpu.VMEM(trace_nodes.shape, jnp.int32),
            pltpu.VMEM(trace_weight.shape, jnp.float32),
            pltpu.SMEM((device_count,), jnp.int32),
            pltpu.SemaphoreType.DMA((5,)),
        ],
        compiler_params=params,
        name="pack_ends",
    )(*hbm(end_device.T, end_local.T, trace_nodes, trace_weight, flat(aperture)))
    values_shape = pltpu.VMEM((device_count, 1, width), jnp.float32)
    (
        values, row_hot, col_hot, col, weight, count, peer, parts, adjoint, source_here, pressure_here,
    ) = pl.pallas_call(
        functools.partial(first_kernel, grid_size),
        out_shape=[
            values_shape,
            pltpu.VMEM((blocks, rows, per_block * width), jnp.bfloat16),
            pltpu.VMEM((blocks, cols, per_block * width), jnp.bfloat16),
            ends_int,
            ends_float,
            pltpu.VMEM((device_count, width), jnp.int32),
            ends_int,
            pltpu.VMEM((5, rows, cols), jnp.float32),
        ]
        + [field] * 3,
        in_specs=[in_vmem] * 2 + [in_hbm] * 2,
        out_specs=[in_vmem] * 11,
        scratch_shapes=[ends_int, field] + leaving + [pltpu.SemaphoreType.DMA((2,))],
        compiler_params=params,
        name="first_values",
    )(*vmem(exchange(message), aperture_here), *hbm(flat(adj_source), flat(pressure)))
    for _ in range(SWEEPS - 1):
        values, adjoint = pl.pallas_call(
            sweep_kernel,
            out_shape=[values_shape, field],
            in_specs=[in_vmem] * 10,
            out_specs=[in_vmem] * 2,
            scratch_shapes=sweeping + leaving,
            compiler_params=params,
            name="sweep",
        )(
            *vmem(
                exchange(values), row_hot, col_hot, col, weight, count, peer, parts, adjoint, source_here
            )
        )
    gradient, adjoint = pl.pallas_call(
        functools.partial(last_kernel, grid_size),
        out_shape=[jax.ShapeDtypeStruct((rows, cols), jnp.float32)] * 2,
        in_specs=[in_vmem] * 11,
        out_specs=[in_hbm] * 2,
        scratch_shapes=sweeping
        + [pltpu.VMEM((4, rows, cols), jnp.float32), field, field, pltpu.SemaphoreType.DMA((2,))],
        compiler_params=params,
        name="last_sweep",
    )(
        *vmem(
            exchange(values), row_hot, col_hot, weight, count, peer, parts, adjoint,
            source_here, aperture_here, pressure_here,
        )
    )
    return gradient.reshape(aperture.shape), adjoint.reshape(aperture.shape)


def solution(mesh):
    fields, pairs = P(AXES, None, None), P(AXES, None)
    return jax.shard_map(
        body,
        mesh=mesh,
        in_specs=(fields, fields, fields, pairs, pairs, pairs, fields),
        out_specs=(fields, fields),
        check_vma=False,
    )
```

```python
import functools
import math

import jax
import jax.numpy as jnp
from jax import lax
from jax.experimental import pallas as pl
from jax.experimental.pallas import tpu as pltpu
from jax.sharding import PartitionSpec as P

SWEEPS = 3
INNER = 8
LEAKAGE = 0.25
AXES = ("wide", "narrow")
SLICE = 8


def start_copies(pairs, sems):
    copies = [
        pltpu.make_async_copy(source, target, sems.at[index]) for index, (source, target) in enumerate(pairs)
    ]
    for copy in copies:
        copy.start()
    return copies


def pack_kernel(
    cells_per, dest_hbm, local_hbm, nodes_hbm, weight_hbm, aperture_hbm,
    out_ref, aperture_ref, dest_ref, local_ref, nodes_ref, weight_ref, seen_ref, sems,
):
    owned = nodes_ref.shape[0]
    devices, _, width = out_ref.shape
    rows = aperture_ref.shape[0]
    copies = start_copies(
        (
            (dest_hbm, dest_ref), (local_hbm, local_ref), (nodes_hbm, nodes_ref), (weight_hbm, weight_ref),
        )
        + tuple(
            (aperture_hbm.at[pl.ds(first, rows // 4)], aperture_ref.at[pl.ds(first, rows // 4)])
            for first in range(0, rows, rows // 4)
        ),
        sems,
    )

    def clear(device, carry):
        seen_ref[device] = 0
        return carry

    lax.fori_loop(0, devices, clear, 0, unroll=8)
    out_ref[:, 0:2, :] = jnp.zeros((devices, 2, width), jnp.float32)
    out_ref[:, 2:4, :] = jnp.full((devices, 2, width), -1.0, jnp.float32)
    for copy in copies[:4]:
        copy.wait()

    def place(index, carry):
        ends = [dest_ref[0, index], dest_ref[1, index]]
        weights = weight_ref[pl.ds(index, 1), :]
        for side in range(2):
            target = ends[side]
            rank = seen_ref[target]
            seen_ref[target] = rank + 1
            first = local_ref[side, index] * cells_per + 1
            cells = (nodes_ref[index, side : side + 1, :] + first).astype(jnp.float32)
            out_ref[target, pl.ds(rank, 1), :] = jnp.concatenate([cells, weights], axis=1)
            out_ref[target, pl.ds(rank + 2, 1), :] = jnp.full(
                (1, width), ends[1 - side].astype(jnp.float32)
            )
        return carry

    lax.fori_loop(0, owned, place, 0, unroll=True)
    for copy in copies[4:]:
        copy.wait()


def face_parts(conduct, grid_size):
    rows, cols = conduct.shape
    row = lax.broadcasted_iota(jnp.int32, (rows, cols), 0) & (grid_size - 1)
    col = lax.broadcasted_iota(jnp.int32, (rows, cols), 1)
    below = jnp.where(row < grid_size - 1, (conduct + pltpu.roll(conduct, rows - 1, 0)) * 0.5, 0.0)
    above = jnp.where(row > 0, (conduct + pltpu.roll(conduct, 1, 0)) * 0.5, 0.0)
    right = jnp.where(col < cols - 1, (conduct + pltpu.roll(conduct, cols - 1, 1)) * 0.5, 0.0)
    left = jnp.where(col > 0, (conduct + pltpu.roll(conduct, 1, 1)) * 0.5, 0.0)
    return below, above, right, left


def split_pair(values):
    high_part = values.astype(jnp.bfloat16)
    low_part = (values - high_part.astype(jnp.float32)).astype(jnp.bfloat16)
    return high_part, low_part


def split_three(values):
    high_part, low_part = split_pair(values)
    rest = values - high_part.astype(jnp.float32) - low_part.astype(jnp.float32)
    return high_part, low_part, rest.astype(jnp.bfloat16)


def over_blocks(count_ref, blocks, work):
    per_block = count_ref.shape[0] // blocks
    work(0)
    if blocks > 1:
        needed = lax.div(count_ref[0, 0] + (per_block - 1), per_block)

        def step(block, carry):
            work(block)
            return carry

        lax.fori_loop(1, needed, step, 0)


def spread(row_hot_ref, col_hot_ref, total_ref, value_of, block):
    _, cols, lanes = col_hot_ref.shape
    group = 2
    width = value_of(block, 0).shape[1]
    total = None
    for start in range(0, lanes // width, group):
        parts = [[], []]
        for device in range(start, start + group):
            hot = col_hot_ref[block, :, device * width : (device + 1) * width]
            for part, value in zip(parts, split_pair(value_of(block, device)), strict=True):
                part.append(hot * value)
        right = jnp.concatenate([jnp.concatenate(part, axis=1) for part in parts], axis=0)
        product = lax.dot_general(
            row_hot_ref[block, :, start * width : (start + group) * width],
            right,
            (((1,), (1,)), ((), ())),
            preferred_element_type=jnp.float32,
        )
        total = product if total is None else total + product
    total = total[:, :cols] + total[:, cols:]
    if isinstance(block, int):
        total_ref[...] = total
    else:
        total_ref[...] += total


def gather(row_hot_ref, col_ref, peer_ref, both_ref, values_ref, block):
    _, per_block, width = col_ref.shape
    cols = both_ref.shape[0] // 2
    group = 2
    col_ids = lax.broadcasted_iota(jnp.int32, (cols, width), 0)
    both = both_ref[...]
    for start in range(0, per_block, group):
        picked = jnp.dot(
            both,
            row_hot_ref[block, :, start * width : (start + group) * width],
            preferred_element_type=jnp.float32,
        )
        picked = picked[:cols] + picked[cols:]
        for offset in range(group):
            device = start + offset
            mine = picked[:, offset * width : (offset + 1) * width]
            hit = col_ids == col_ref[block, device : device + 1, :]
            values_ref[peer_ref[block, device, 0]] = jnp.sum(
                jnp.where(hit, mine, 0.0), axis=0, keepdims=True
            )


def send_values(adjoint, row_hot_ref, col_ref, count_ref, peer_ref, both_ref, values_ref):
    values_ref[...] = jnp.zeros(values_ref.shape, jnp.float32)
    both_ref[...] = jnp.concatenate(split_pair(adjoint.T), axis=0)
    over_blocks(
        count_ref, col_ref.shape[0],
        lambda block: gather(row_hot_ref, col_ref, peer_ref, both_ref, values_ref, block),
    )


def first_kernel(
    grid_size, message_ref, aperture_ref, source_hbm, pressure_hbm,
    values_ref, row_hot_ref, col_hot_ref, col_ref, weight_ref, count_ref, peer_ref, parts_ref, adjoint_ref,
    source_ref, pressure_ref, row_ref, total_ref, both_ref, sems,
):
    copies = start_copies(
        ((source_hbm, source_ref), (pressure_hbm, pressure_ref)), sems
    )
    devices, _, width = message_ref.shape
    trace_len = width // 2
    blocks, per_block, _ = col_ref.shape
    rows, cols = aperture_ref.shape
    aperture = aperture_ref[...]
    faces = face_parts(aperture * aperture * aperture / 12.0, grid_size)
    for index in range(4):
        parts_ref[index] = faces[index]
    parts_ref[4] = LEAKAGE + (faces[0] + faces[1] + faces[2] + faces[3])
    slots = [message_ref[:, rank, :] for rank in range(2)]
    partners = [message_ref[:, 2 + rank, :] for rank in range(2)]
    down = lax.broadcasted_iota(jnp.int32, (devices, width), 0)
    along = lax.broadcasted_iota(jnp.int32, (devices, width), 1)
    device_id = down.astype(jnp.float32)
    target = [
        jnp.sum(jnp.where(down == along, partners[rank], 0.0), axis=0, keepdims=True) for rank in range(2)
    ]
    target = [jnp.where(along[0:1] < devices, target[rank], -1.0) for rank in range(2)]
    used = jnp.where((device_id == target[0]) | (device_id == target[1]), 1.0, 0.0)
    used = jnp.max(used, axis=1, keepdims=True)
    count = jnp.sum(used, axis=0, keepdims=True)
    packed = jnp.zeros((2 * devices, 4 * width), jnp.float32)
    for rank in range(2):
        place = jnp.sum(jnp.where(device_id < target[rank], used, 0.0), axis=0, keepdims=True)
        ahead = (down < along) if rank == 0 else (down <= along)
        earlier = jnp.where((partners[0] == target[rank]) & ahead, 1.0, 0.0)
        earlier = earlier + jnp.where((partners[1] == target[rank]) & (down < along), 1.0, 0.0)
        spot = jnp.sum(earlier, axis=0, keepdims=True)
        here = (device_id == place) & (target[rank] >= 0.0)
        pick = [jnp.where(here & (spot == float(index)), 1.0, 0.0).astype(jnp.bfloat16) for index in range(2)]
        packed = packed + jnp.dot(
            jnp.concatenate(pick, axis=0)[:, :devices],
            jnp.concatenate(split_three(slots[rank]) + (partners[rank].astype(jnp.bfloat16),), axis=1),
            preferred_element_type=jnp.float32,
        )
    ends = packed[:, :width] + packed[:, width : 2 * width] + packed[:, 2 * width : 3 * width]
    ends = [ends[:devices], ends[devices:]]
    front = along < trace_len
    cell = jnp.where(front, ends[0], pltpu.roll(ends[1], trace_len, 1)).astype(jnp.int32) - 1
    weight = jnp.where(front, pltpu.roll(ends[0], trace_len, 1), ends[1])
    me = lax.axis_index(AXES)
    peer = jnp.where(device_id < count, packed[:devices, 3 * width :].astype(jnp.int32), me)
    count_ref[...] = jnp.broadcast_to(count, count_ref.shape).astype(jnp.int32)
    peer_ref[...] = peer.reshape(peer_ref.shape)
    weight_ref[...] = weight.reshape(weight_ref.shape)
    row_ref[...] = (cell >> (grid_size.bit_length() - 1)).reshape(row_ref.shape)
    col_ref[...] = (cell & (grid_size - 1)).reshape(col_ref.shape)
    cell_ids = lax.broadcasted_iota(jnp.int32, (rows, width), 0).astype(jnp.float32).astype(jnp.bfloat16)
    one, zero = jnp.ones((), jnp.bfloat16), jnp.zeros((), jnp.bfloat16)

    def build(block):
        block_cols = col_ref[block].astype(jnp.float32).astype(jnp.bfloat16)
        block_rows = row_ref[block].astype(jnp.float32).astype(jnp.bfloat16)
        for device in range(per_block):
            lanes = slice(device * width, (device + 1) * width)
            row_hot_ref[block, :, lanes] = jnp.where(cell_ids == block_rows[device : device + 1], one, zero)
            col_hot_ref[block, :, lanes] = jnp.where(
                cell_ids[:cols] == block_cols[device : device + 1], one, zero
            )
        spread(
            row_hot_ref, col_hot_ref, total_ref,
            lambda block, device: weight_ref[block, device : device + 1, :], block,
        )

    over_blocks(count_ref, blocks, build)
    inv_diag = 1.0 / (parts_ref[4] + total_ref[...])
    for copy in copies:
        copy.wait()
    parts_ref[4] = inv_diag
    adjoint = source_ref[...] * inv_diag
    adjoint_ref[...] = adjoint
    send_values(adjoint, row_hot_ref, col_ref, count_ref, peer_ref, both_ref, values_ref)


def near(state_ref, rows):
    cols = state_ref.shape[1]
    first = SLICE + rows
    here = state_ref[first : first + SLICE]
    return here, (
        state_ref[first + 1 : first + SLICE + 1],
        state_ref[first - 1 : first + SLICE - 1],
        pltpu.roll(here, cols - 1, 1),
        pltpu.roll(here, 1, 1),
    )


def relax(
    arrived_ref, row_hot_ref, col_hot_ref, weight_ref, count_ref, peer_ref, parts_ref, start_ref, source_ref,
    adjoint_ref, total_ref, early_ref, state_ref, before_ref=None,
):
    rows, cols = start_ref.shape
    slices = range(0, rows, SLICE)
    margin = jnp.zeros((SLICE, cols), jnp.float32)
    for index in range(2):
        state_ref[index, 0:SLICE] = margin
        state_ref[index, SLICE + rows :] = margin
    state_ref[0, SLICE : SLICE + rows] = start_ref[...]

    def pull(state, first):
        _, (below, above, right, left) = near(state, first)
        here = slice(first, first + SLICE)
        return (parts_ref[0, here] * below + parts_ref[1, here] * above) + (
            parts_ref[2, here] * right + parts_ref[3, here] * left
        )

    for first in slices:
        early_ref[first : first + SLICE] = pull(state_ref.at[0], first)
    if before_ref is not None:
        before_ref()
    over_blocks(
        count_ref, weight_ref.shape[0],
        lambda block: spread(
            row_hot_ref, col_hot_ref, total_ref,
            lambda block, device: weight_ref[block, device : device + 1, :] * arrived_ref[peer_ref[block, device, 0]],
            block,
        ),
    )
    for step in range(INNER):
        old, new = state_ref.at[step % 2], state_ref.at[(step + 1) % 2]
        for first in slices:
            here = slice(first, first + SLICE)
            if step == 0:
                forcing = source_ref[here] + total_ref[here]
                total_ref[here] = forcing
                now = (forcing + early_ref[here]) * parts_ref[4, here]
            else:
                now = (total_ref[here] + pull(old, first)) * parts_ref[4, here]
            new[SLICE + first : 2 * SLICE + first] = now
            if step == INNER - 1:
                adjoint_ref[here] = now


def sweep_kernel(
    arrived_ref, row_hot_ref, col_hot_ref, col_ref, weight_ref, count_ref, peer_ref, parts_ref, start_ref,
    source_ref, values_ref, adjoint_ref, total_ref, early_ref, state_ref, both_ref,
):
    relax(
        arrived_ref, row_hot_ref, col_hot_ref, weight_ref, count_ref, peer_ref, parts_ref, start_ref, source_ref,
        adjoint_ref, total_ref, early_ref, state_ref,
    )
    send_values(adjoint_ref[...], row_hot_ref, col_ref, count_ref, peer_ref, both_ref, values_ref)


def last_kernel(
    grid_size, arrived_ref, row_hot_ref, col_hot_ref, weight_ref, count_ref, peer_ref, parts_ref, start_ref,
    source_ref, aperture_ref, pressure_ref, gradient_hbm, adjoint_hbm,
    total_ref, early_ref, state_ref, share_ref, gradient_ref, adjoint_ref, sems,
):
    rows, cols = start_ref.shape
    slices = range(0, rows, SLICE)

    def shares():
        aperture = aperture_ref[...]
        scale = -(aperture * aperture / 8.0)
        pressure = pressure_ref[...]
        row = lax.broadcasted_iota(jnp.int32, (rows, cols), 0) & (grid_size - 1)
        col = lax.broadcasted_iota(jnp.int32, (rows, cols), 1)
        inside = (row < grid_size - 1, row > 0, col < cols - 1, col > 0)
        turns = ((rows - 1, 0), (1, 0), (cols - 1, 1), (1, 1))
        for index in range(4):
            share_ref[index] = jnp.where(
                inside[index], scale * (pressure - pltpu.roll(pressure, *turns[index])), 0.0
            )

    relax(
        arrived_ref, row_hot_ref, col_hot_ref, weight_ref, count_ref, peer_ref, parts_ref, start_ref, source_ref,
        adjoint_ref, total_ref, early_ref, state_ref, shares,
    )
    keep = pltpu.make_async_copy(adjoint_ref, adjoint_hbm, sems.at[0])
    keep.start()
    last_state = state_ref.at[INNER % 2]
    for first in slices:
        here, sides = near(last_state, first)
        lines = slice(first, first + SLICE)
        terms = [share_ref[index, lines] * (here - side) for index, side in enumerate(sides)]
        gradient_ref[lines] = (terms[0] + terms[1]) + (terms[2] + terms[3])
    send = pltpu.make_async_copy(gradient_ref, gradient_hbm, sems.at[1])
    send.start()
    keep.wait()
    send.wait()


def body(aperture, pressure, adj_source, trace_weight, end_device, end_local, trace_nodes):
    frac_count, grid_size, _ = aperture.shape
    owned_count, trace_len = trace_weight.shape
    device_count = lax.axis_size(AXES)
    rows, cols, width = frac_count * grid_size, grid_size, 2 * trace_len
    nodes = device_count * width
    per_block = math.gcd(device_count, 16)
    blocks = device_count // per_block
    in_vmem = pl.BlockSpec(memory_space=pltpu.VMEM)
    in_hbm = pl.BlockSpec(memory_space=pltpu.HBM)
    params = pltpu.CompilerParams(vmem_limit_bytes=(8 << 20) + nodes * 1024)
    field = pltpu.VMEM((rows, cols), jnp.float32)
    sweeping = [field, field, pltpu.VMEM((2, rows + 2 * SLICE, cols), jnp.float32)]
    leaving = [pltpu.VMEM((2 * cols, rows), jnp.bfloat16)]
    ends_int = pltpu.VMEM((blocks, per_block, width), jnp.int32)
    ends_float = pltpu.VMEM((blocks, per_block, width), jnp.float32)

    def flat(whole):
        return whole.reshape(rows, cols)

    def vmem(*arrays):
        return [pltpu.with_memory_space_constraint(array, pltpu.VMEM) for array in arrays]

    def hbm(*arrays):
        return [pltpu.with_memory_space_constraint(array, pltpu.HBM) for array in arrays]

    def exchange(values):
        return lax.all_to_all(values, AXES, split_axis=0, concat_axis=0, tiled=True)

    message, aperture_here = pl.pallas_call(
        functools.partial(pack_kernel, grid_size * grid_size),
        out_shape=[pltpu.VMEM((device_count, 4, width), jnp.float32), field],
        in_specs=[in_hbm] * 5,
        out_specs=[in_vmem] * 2,
        scratch_shapes=[
            pltpu.SMEM((2, owned_count), jnp.int32),
            pltpu.SMEM((2, owned_count), jnp.int32),
            pltpu.VMEM(trace_nodes.shape, jnp.int32),
            pltpu.VMEM(trace_weight.shape, jnp.float32),
            pltpu.SMEM((device_count,), jnp.int32),
            pltpu.SemaphoreType.DMA((8,)),
        ],
        compiler_params=params,
        name="pack_ends",
    )(*hbm(end_device.T, end_local.T, trace_nodes, trace_weight, flat(aperture)))
    values_shape = pltpu.VMEM((device_count, 1, width), jnp.float32)
    (
        values, row_hot, col_hot, col, weight, count, peer, parts, adjoint, source_here, pressure_here,
    ) = pl.pallas_call(
        functools.partial(first_kernel, grid_size),
        out_shape=[
            values_shape,
            pltpu.VMEM((blocks, rows, per_block * width), jnp.bfloat16),
            pltpu.VMEM((blocks, cols, per_block * width), jnp.bfloat16),
            ends_int,
            ends_float,
            pltpu.VMEM((device_count, width), jnp.int32),
            ends_int,
            pltpu.VMEM((5, rows, cols), jnp.float32),
        ]
        + [field] * 3,
        in_specs=[in_vmem] * 2 + [in_hbm] * 2,
        out_specs=[in_vmem] * 11,
        scratch_shapes=[ends_int, field] + leaving + [pltpu.SemaphoreType.DMA((2,))],
        compiler_params=params,
        name="first_values",
    )(*vmem(exchange(message), aperture_here), *hbm(flat(adj_source), flat(pressure)))
    for _ in range(SWEEPS - 1):
        values, adjoint = pl.pallas_call(
            sweep_kernel,
            out_shape=[values_shape, field],
            in_specs=[in_vmem] * 10,
            out_specs=[in_vmem] * 2,
            scratch_shapes=sweeping + leaving,
            compiler_params=params,
            name="sweep",
        )(
            *vmem(
                exchange(values), row_hot, col_hot, col, weight, count, peer, parts, adjoint, source_here
            )
        )
    gradient, adjoint = pl.pallas_call(
        functools.partial(last_kernel, grid_size),
        out_shape=[jax.ShapeDtypeStruct((rows, cols), jnp.float32)] * 2,
        in_specs=[in_vmem] * 11,
        out_specs=[in_hbm] * 2,
        scratch_shapes=sweeping
        + [pltpu.VMEM((4, rows, cols), jnp.float32), field, field, pltpu.SemaphoreType.DMA((2,))],
        compiler_params=params,
        name="last_sweep",
    )(
        *vmem(
            exchange(values), row_hot, col_hot, weight, count, peer, parts, adjoint,
            source_here, aperture_here, pressure_here,
        )
    )
    return gradient.reshape(aperture.shape), adjoint.reshape(aperture.shape)


def solution(mesh):
    fields, pairs = P(AXES, None, None), P(AXES, None)
    return jax.shard_map(
        body,
        mesh=mesh,
        in_specs=(fields, fields, fields, pairs, pairs, pairs, fields),
        out_specs=(fields, fields),
        check_vma=False,
    )
```

```python
import functools
import math

import jax
import jax.numpy as jnp
from jax import lax
from jax.experimental import pallas as pl
from jax.experimental.pallas import tpu as pltpu
from jax.sharding import PartitionSpec as P

SWEEPS = 3
INNER = 8
LEAKAGE = 0.25
AXES = ("wide", "narrow")
SLICE = 8


def start_copies(pairs, sems):
    copies = [
        pltpu.make_async_copy(source, target, sems.at[index]) for index, (source, target) in enumerate(pairs)
    ]
    for copy in copies:
        copy.start()
    return copies


def pack_kernel(
    cells_per, dest_hbm, local_hbm, nodes_hbm, weight_hbm, aperture_hbm,
    out_ref, aperture_ref, dest_ref, local_ref, nodes_ref, weight_ref, seen_ref, sems,
):
    owned = nodes_ref.shape[0]
    devices, _, width = out_ref.shape
    rows = aperture_ref.shape[0]
    copies = start_copies(
        (
            (dest_hbm, dest_ref), (local_hbm, local_ref), (nodes_hbm, nodes_ref), (weight_hbm, weight_ref),
        )
        + tuple(
            (aperture_hbm.at[pl.ds(first, rows // 4)], aperture_ref.at[pl.ds(first, rows // 4)])
            for first in range(0, rows, rows // 4)
        ),
        sems,
    )

    def clear(device, carry):
        seen_ref[device] = 0
        return carry

    lax.fori_loop(0, devices, clear, 0, unroll=8)
    out_ref[:, 0:2, :] = jnp.zeros((devices, 2, width), jnp.float32)
    out_ref[:, 2:4, :] = jnp.full((devices, 2, width), -1.0, jnp.float32)
    for copy in copies[:4]:
        copy.wait()

    def place(index, carry):
        ends = [dest_ref[0, index], dest_ref[1, index]]
        weights = weight_ref[pl.ds(index, 1), :]
        for side in range(2):
            target = ends[side]
            rank = seen_ref[target]
            seen_ref[target] = rank + 1
            first = local_ref[side, index] * cells_per + 1
            cells = (nodes_ref[index, side : side + 1, :] + first).astype(jnp.float32)
            out_ref[target, pl.ds(rank, 1), :] = jnp.concatenate([cells, weights], axis=1)
            out_ref[target, pl.ds(rank + 2, 1), :] = jnp.full(
                (1, width), ends[1 - side].astype(jnp.float32)
            )
        return carry

    lax.fori_loop(0, owned, place, 0, unroll=True)
    for copy in copies[4:]:
        copy.wait()


def face_parts(conduct, grid_size):
    rows, cols = conduct.shape
    row = lax.broadcasted_iota(jnp.int32, (rows, cols), 0) & (grid_size - 1)
    col = lax.broadcasted_iota(jnp.int32, (rows, cols), 1)
    below = jnp.where(row < grid_size - 1, (conduct + pltpu.roll(conduct, rows - 1, 0)) * 0.5, 0.0)
    above = jnp.where(row > 0, (conduct + pltpu.roll(conduct, 1, 0)) * 0.5, 0.0)
    right = jnp.where(col < cols - 1, (conduct + pltpu.roll(conduct, cols - 1, 1)) * 0.5, 0.0)
    left = jnp.where(col > 0, (conduct + pltpu.roll(conduct, 1, 1)) * 0.5, 0.0)
    return below, above, right, left


def split_pair(values):
    high_part = values.astype(jnp.bfloat16)
    low_part = (values - high_part.astype(jnp.float32)).astype(jnp.bfloat16)
    return high_part, low_part


def split_three(values):
    high_part, low_part = split_pair(values)
    rest = values - high_part.astype(jnp.float32) - low_part.astype(jnp.float32)
    return high_part, low_part, rest.astype(jnp.bfloat16)


def over_blocks(count_ref, blocks, work):
    per_block = count_ref.shape[0] // blocks
    work(0)
    if blocks > 1:
        needed = lax.div(count_ref[0, 0] + (per_block - 1), per_block)

        def step(block, carry):
            work(block)
            return carry

        lax.fori_loop(1, needed, step, 0)


def spread(row_hot_ref, col_hot_ref, total_ref, value_of, block):
    _, cols, lanes = col_hot_ref.shape
    group = 2
    width = value_of(block, 0).shape[1]
    total = None
    for start in range(0, lanes // width, group):
        parts = [[], []]
        for device in range(start, start + group):
            hot = col_hot_ref[block, :, device * width : (device + 1) * width]
            for part, value in zip(parts, split_pair(value_of(block, device)), strict=True):
                part.append(hot * value)
        right = jnp.concatenate([jnp.concatenate(part, axis=1) for part in parts], axis=0)
        product = lax.dot_general(
            row_hot_ref[block, :, start * width : (start + group) * width],
            right,
            (((1,), (1,)), ((), ())),
            preferred_element_type=jnp.float32,
        )
        total = product if total is None else total + product
    total = total[:, :cols] + total[:, cols:]
    if isinstance(block, int):
        total_ref[...] = total
    else:
        total_ref[...] += total


def gather(col_hot_ref, row_ref, peer_ref, both_ref, values_ref, block):
    _, per_block, width = row_ref.shape
    rows = both_ref.shape[0]
    group = 2
    row_ids = lax.broadcasted_iota(jnp.int32, (rows, width), 0)
    both = both_ref[...]
    for start in range(0, per_block, group):
        hot = col_hot_ref[block, :, start * width : (start + group) * width]
        picked = jnp.dot(both, jnp.concatenate([hot, hot], axis=0), preferred_element_type=jnp.float32)
        for offset in range(group):
            device = start + offset
            mine = picked[:, offset * width : (offset + 1) * width]
            hit = row_ids == row_ref[block, device : device + 1, :]
            values_ref[peer_ref[block, device, 0]] = jnp.sum(
                jnp.where(hit, mine, 0.0), axis=0, keepdims=True
            )


def send_values(adjoint, col_hot_ref, row_ref, count_ref, peer_ref, both_ref, values_ref):
    values_ref[...] = jnp.zeros(values_ref.shape, jnp.float32)
    both_ref[...] = jnp.concatenate(split_pair(adjoint), axis=1)
    over_blocks(
        count_ref, row_ref.shape[0],
        lambda block: gather(col_hot_ref, row_ref, peer_ref, both_ref, values_ref, block),
    )


def first_kernel(
    grid_size, message_ref, aperture_ref, source_hbm, pressure_hbm,
    values_ref, row_hot_ref, col_hot_ref, row_ref, weight_ref, count_ref, peer_ref, parts_ref, adjoint_ref,
    source_ref, pressure_ref, col_ref, total_ref, both_ref, sems,
):
    copies = start_copies(
        ((source_hbm, source_ref), (pressure_hbm, pressure_ref)), sems
    )
    devices, _, width = message_ref.shape
    trace_len = width // 2
    blocks, per_block, _ = col_ref.shape
    rows, cols = aperture_ref.shape
    aperture = aperture_ref[...]
    faces = face_parts(aperture * aperture * aperture / 12.0, grid_size)
    for index in range(4):
        parts_ref[index] = faces[index]
    parts_ref[4] = LEAKAGE + (faces[0] + faces[1] + faces[2] + faces[3])
    slots = [message_ref[:, rank, :] for rank in range(2)]
    partners = [message_ref[:, 2 + rank, :] for rank in range(2)]
    down = lax.broadcasted_iota(jnp.int32, (devices, width), 0)
    along = lax.broadcasted_iota(jnp.int32, (devices, width), 1)
    device_id = down.astype(jnp.float32)
    target = [
        jnp.sum(jnp.where(down == along, partners[rank], 0.0), axis=0, keepdims=True) for rank in range(2)
    ]
    target = [jnp.where(along[0:1] < devices, target[rank], -1.0) for rank in range(2)]
    used = jnp.where((device_id == target[0]) | (device_id == target[1]), 1.0, 0.0)
    used = jnp.max(used, axis=1, keepdims=True)
    count = jnp.sum(used, axis=0, keepdims=True)
    packed = jnp.zeros((2 * devices, 4 * width), jnp.float32)
    for rank in range(2):
        place = jnp.sum(jnp.where(device_id < target[rank], used, 0.0), axis=0, keepdims=True)
        ahead = (down < along) if rank == 0 else (down <= along)
        earlier = jnp.where((partners[0] == target[rank]) & ahead, 1.0, 0.0)
        earlier = earlier + jnp.where((partners[1] == target[rank]) & (down < along), 1.0, 0.0)
        spot = jnp.sum(earlier, axis=0, keepdims=True)
        here = (device_id == place) & (target[rank] >= 0.0)
        pick = [jnp.where(here & (spot == float(index)), 1.0, 0.0).astype(jnp.bfloat16) for index in range(2)]
        packed = packed + jnp.dot(
            jnp.concatenate(pick, axis=0)[:, :devices],
            jnp.concatenate(split_three(slots[rank]) + (partners[rank].astype(jnp.bfloat16),), axis=1),
            preferred_element_type=jnp.float32,
        )
    ends = packed[:, :width] + packed[:, width : 2 * width] + packed[:, 2 * width : 3 * width]
    ends = [ends[:devices], ends[devices:]]
    front = along < trace_len
    cell = jnp.where(front, ends[0], pltpu.roll(ends[1], trace_len, 1)).astype(jnp.int32) - 1
    weight = jnp.where(front, pltpu.roll(ends[0], trace_len, 1), ends[1])
    me = lax.axis_index(AXES)
    peer = jnp.where(device_id < count, packed[:devices, 3 * width :].astype(jnp.int32), me)
    count_ref[...] = jnp.broadcast_to(count, count_ref.shape).astype(jnp.int32)
    peer_ref[...] = peer.reshape(peer_ref.shape)
    weight_ref[...] = weight.reshape(weight_ref.shape)
    row_ref[...] = (cell >> (grid_size.bit_length() - 1)).reshape(row_ref.shape)
    col_ref[...] = (cell & (grid_size - 1)).reshape(col_ref.shape)
    cell_ids = lax.broadcasted_iota(jnp.int32, (rows, width), 0).astype(jnp.float32).astype(jnp.bfloat16)
    one, zero = jnp.ones((), jnp.bfloat16), jnp.zeros((), jnp.bfloat16)

    def build(block):
        block_cols = col_ref[block].astype(jnp.float32).astype(jnp.bfloat16)
        block_rows = row_ref[block].astype(jnp.float32).astype(jnp.bfloat16)
        for device in range(per_block):
            lanes = slice(device * width, (device + 1) * width)
            row_hot_ref[block, :, lanes] = jnp.where(cell_ids == block_rows[device : device + 1], one, zero)
            col_hot_ref[block, :, lanes] = jnp.where(
                cell_ids[:cols] == block_cols[device : device + 1], one, zero
            )
        spread(
            row_hot_ref, col_hot_ref, total_ref,
            lambda block, device: weight_ref[block, device : device + 1, :], block,
        )

    over_blocks(count_ref, blocks, build)
    inv_diag = 1.0 / (parts_ref[4] + total_ref[...])
    for copy in copies:
        copy.wait()
    parts_ref[4] = inv_diag
    adjoint = source_ref[...] * inv_diag
    adjoint_ref[...] = adjoint
    send_values(adjoint, col_hot_ref, row_ref, count_ref, peer_ref, both_ref, values_ref)


def near(state_ref, rows):
    cols = state_ref.shape[1]
    first = SLICE + rows
    here = state_ref[first : first + SLICE]
    return here, (
        state_ref[first + 1 : first + SLICE + 1],
        state_ref[first - 1 : first + SLICE - 1],
        pltpu.roll(here, cols - 1, 1),
        pltpu.roll(here, 1, 1),
    )


def relax(
    arrived_ref, row_hot_ref, col_hot_ref, weight_ref, count_ref, peer_ref, parts_ref, start_ref, source_ref,
    adjoint_ref, total_ref, early_ref, state_ref, before_ref=None,
):
    rows, cols = start_ref.shape
    slices = range(0, rows, SLICE)
    margin = jnp.zeros((SLICE, cols), jnp.float32)
    for index in range(2):
        state_ref[index, 0:SLICE] = margin
        state_ref[index, SLICE + rows :] = margin
    state_ref[0, SLICE : SLICE + rows] = start_ref[...]

    def pull(state, first):
        _, (below, above, right, left) = near(state, first)
        here = slice(first, first + SLICE)
        return (parts_ref[0, here] * below + parts_ref[1, here] * above) + (
            parts_ref[2, here] * right + parts_ref[3, here] * left
        )

    for first in slices:
        early_ref[first : first + SLICE] = pull(state_ref.at[0], first)
    if before_ref is not None:
        before_ref()
    over_blocks(
        count_ref, weight_ref.shape[0],
        lambda block: spread(
            row_hot_ref, col_hot_ref, total_ref,
            lambda block, device: weight_ref[block, device : device + 1, :] * arrived_ref[peer_ref[block, device, 0]],
            block,
        ),
    )
    for step in range(INNER):
        old, new = state_ref.at[step % 2], state_ref.at[(step + 1) % 2]
        for first in slices:
            here = slice(first, first + SLICE)
            if step == 0:
                forcing = source_ref[here] + total_ref[here]
                total_ref[here] = forcing
                now = (forcing + early_ref[here]) * parts_ref[4, here]
            else:
                now = (total_ref[here] + pull(old, first)) * parts_ref[4, here]
            new[SLICE + first : 2 * SLICE + first] = now
            if step == INNER - 1:
                adjoint_ref[here] = now


def sweep_kernel(
    arrived_ref, row_hot_ref, col_hot_ref, row_ref, weight_ref, count_ref, peer_ref, parts_ref, start_ref,
    source_ref, values_ref, adjoint_ref, total_ref, early_ref, state_ref, both_ref,
):
    relax(
        arrived_ref, row_hot_ref, col_hot_ref, weight_ref, count_ref, peer_ref, parts_ref, start_ref, source_ref,
        adjoint_ref, total_ref, early_ref, state_ref,
    )
    send_values(adjoint_ref[...], col_hot_ref, row_ref, count_ref, peer_ref, both_ref, values_ref)


def last_kernel(
    grid_size, arrived_ref, row_hot_ref, col_hot_ref, weight_ref, count_ref, peer_ref, parts_ref, start_ref,
    source_ref, aperture_ref, pressure_ref, gradient_hbm, adjoint_hbm,
    total_ref, early_ref, state_ref, share_ref, gradient_ref, adjoint_ref, sems,
):
    rows, cols = start_ref.shape
    slices = range(0, rows, SLICE)

    def shares():
        aperture = aperture_ref[...]
        scale = -(aperture * aperture / 8.0)
        pressure = pressure_ref[...]
        row = lax.broadcasted_iota(jnp.int32, (rows, cols), 0) & (grid_size - 1)
        col = lax.broadcasted_iota(jnp.int32, (rows, cols), 1)
        inside = (row < grid_size - 1, row > 0, col < cols - 1, col > 0)
        turns = ((rows - 1, 0), (1, 0), (cols - 1, 1), (1, 1))
        for index in range(4):
            share_ref[index] = jnp.where(
                inside[index], scale * (pressure - pltpu.roll(pressure, *turns[index])), 0.0
            )

    relax(
        arrived_ref, row_hot_ref, col_hot_ref, weight_ref, count_ref, peer_ref, parts_ref, start_ref, source_ref,
        adjoint_ref, total_ref, early_ref, state_ref, shares,
    )
    keep = pltpu.make_async_copy(adjoint_ref, adjoint_hbm, sems.at[0])
    keep.start()
    last_state = state_ref.at[INNER % 2]
    for first in slices:
        here, sides = near(last_state, first)
        lines = slice(first, first + SLICE)
        terms = [share_ref[index, lines] * (here - side) for index, side in enumerate(sides)]
        gradient_ref[lines] = (terms[0] + terms[1]) + (terms[2] + terms[3])
    send = pltpu.make_async_copy(gradient_ref, gradient_hbm, sems.at[1])
    send.start()
    keep.wait()
    send.wait()


def body(aperture, pressure, adj_source, trace_weight, end_device, end_local, trace_nodes):
    frac_count, grid_size, _ = aperture.shape
    owned_count, trace_len = trace_weight.shape
    device_count = lax.axis_size(AXES)
    rows, cols, width = frac_count * grid_size, grid_size, 2 * trace_len
    nodes = device_count * width
    per_block = math.gcd(device_count, 16)
    blocks = device_count // per_block
    in_vmem = pl.BlockSpec(memory_space=pltpu.VMEM)
    in_hbm = pl.BlockSpec(memory_space=pltpu.HBM)
    params = pltpu.CompilerParams(vmem_limit_bytes=(8 << 20) + nodes * 1024)
    field = pltpu.VMEM((rows, cols), jnp.float32)
    sweeping = [field, field, pltpu.VMEM((2, rows + 2 * SLICE, cols), jnp.float32)]
    leaving = [pltpu.VMEM((rows, 2 * cols), jnp.bfloat16)]
    ends_int = pltpu.VMEM((blocks, per_block, width), jnp.int32)
    ends_float = pltpu.VMEM((blocks, per_block, width), jnp.float32)

    def flat(whole):
        return whole.reshape(rows, cols)

    def vmem(*arrays):
        return [pltpu.with_memory_space_constraint(array, pltpu.VMEM) for array in arrays]

    def hbm(*arrays):
        return [pltpu.with_memory_space_constraint(array, pltpu.HBM) for array in arrays]

    def exchange(values):
        return lax.all_to_all(values, AXES, split_axis=0, concat_axis=0, tiled=True)

    message, aperture_here = pl.pallas_call(
        functools.partial(pack_kernel, grid_size * grid_size),
        out_shape=[pltpu.VMEM((device_count, 4, width), jnp.float32), field],
        in_specs=[in_hbm] * 5,
        out_specs=[in_vmem] * 2,
        scratch_shapes=[
            pltpu.SMEM((2, owned_count), jnp.int32),
            pltpu.SMEM((2, owned_count), jnp.int32),
            pltpu.VMEM(trace_nodes.shape, jnp.int32),
            pltpu.VMEM(trace_weight.shape, jnp.float32),
            pltpu.SMEM((device_count,), jnp.int32),
            pltpu.SemaphoreType.DMA((8,)),
        ],
        compiler_params=params,
        name="pack_ends",
    )(*hbm(end_device.T, end_local.T, trace_nodes, trace_weight, flat(aperture)))
    values_shape = pltpu.VMEM((device_count, 1, width), jnp.float32)
    (
        values, row_hot, col_hot, row, weight, count, peer, parts, adjoint, source_here, pressure_here,
    ) = pl.pallas_call(
        functools.partial(first_kernel, grid_size),
        out_shape=[
            values_shape,
            pltpu.VMEM((blocks, rows, per_block * width), jnp.bfloat16),
            pltpu.VMEM((blocks, cols, per_block * width), jnp.bfloat16),
            ends_int,
            ends_float,
            pltpu.VMEM((device_count, width), jnp.int32),
            ends_int,
            pltpu.VMEM((5, rows, cols), jnp.float32),
        ]
        + [field] * 3,
        in_specs=[in_vmem] * 2 + [in_hbm] * 2,
        out_specs=[in_vmem] * 11,
        scratch_shapes=[ends_int, field] + leaving + [pltpu.SemaphoreType.DMA((2,))],
        compiler_params=params,
        name="first_values",
    )(*vmem(exchange(message), aperture_here), *hbm(flat(adj_source), flat(pressure)))
    for _ in range(SWEEPS - 1):
        values, adjoint = pl.pallas_call(
            sweep_kernel,
            out_shape=[values_shape, field],
            in_specs=[in_vmem] * 10,
            out_specs=[in_vmem] * 2,
            scratch_shapes=sweeping + leaving,
            compiler_params=params,
            name="sweep",
        )(
            *vmem(
                exchange(values), row_hot, col_hot, row, weight, count, peer, parts, adjoint, source_here
            )
        )
    gradient, adjoint = pl.pallas_call(
        functools.partial(last_kernel, grid_size),
        out_shape=[jax.ShapeDtypeStruct((rows, cols), jnp.float32)] * 2,
        in_specs=[in_vmem] * 11,
        out_specs=[in_hbm] * 2,
        scratch_shapes=sweeping
        + [pltpu.VMEM((4, rows, cols), jnp.float32), field, field, pltpu.SemaphoreType.DMA((2,))],
        compiler_params=params,
        name="last_sweep",
    )(
        *vmem(
            exchange(values), row_hot, col_hot, weight, count, peer, parts, adjoint,
            source_here, aperture_here, pressure_here,
        )
    )
    return gradient.reshape(aperture.shape), adjoint.reshape(aperture.shape)


def solution(mesh):
    fields, pairs = P(AXES, None, None), P(AXES, None)
    return jax.shard_map(
        body,
        mesh=mesh,
        in_specs=(fields, fields, fields, pairs, pairs, pairs, fields),
        out_specs=(fields, fields),
        check_vma=False,
    )
```

```python
import functools
import math

import jax
import jax.numpy as jnp
from jax import lax
from jax.experimental import pallas as pl
from jax.experimental.pallas import tpu as pltpu
from jax.sharding import PartitionSpec as P

SWEEPS = 3
INNER = 8
LEAKAGE = 0.25
AXES = ("wide", "narrow")
SLICE = 8


def start_copies(pairs, sems):
    copies = [
        pltpu.make_async_copy(source, target, sems.at[index]) for index, (source, target) in enumerate(pairs)
    ]
    for copy in copies:
        copy.start()
    return copies


def pack_kernel(
    cells_per, dest_hbm, local_hbm, nodes_hbm, weight_hbm, aperture_hbm,
    out_ref, aperture_ref, dest_ref, local_ref, nodes_ref, weight_ref, seen_ref, sems,
):
    owned = nodes_ref.shape[0]
    devices, _, width = out_ref.shape
    rows = aperture_ref.shape[0]
    copies = start_copies(
        (
            (dest_hbm, dest_ref), (local_hbm, local_ref), (nodes_hbm, nodes_ref), (weight_hbm, weight_ref),
        )
        + tuple(
            (aperture_hbm.at[pl.ds(first, rows // 4)], aperture_ref.at[pl.ds(first, rows // 4)])
            for first in range(0, rows, rows // 4)
        ),
        sems,
    )

    def clear(device, carry):
        seen_ref[device] = 0
        return carry

    lax.fori_loop(0, devices, clear, 0, unroll=8)
    out_ref[:, 0:2, :] = jnp.zeros((devices, 2, width), jnp.float32)
    out_ref[:, 2:4, :] = jnp.full((devices, 2, width), -1.0, jnp.float32)
    for copy in copies[:4]:
        copy.wait()

    def place(index, carry):
        ends = [dest_ref[0, index], dest_ref[1, index]]
        weights = weight_ref[pl.ds(index, 1), :]
        for side in range(2):
            target = ends[side]
            rank = seen_ref[target]
            seen_ref[target] = rank + 1
            first = local_ref[side, index] * cells_per + 1
            cells = (nodes_ref[index, side : side + 1, :] + first).astype(jnp.float32)
            out_ref[target, pl.ds(rank, 1), :] = jnp.concatenate([cells, weights], axis=1)
            out_ref[target, pl.ds(rank + 2, 1), :] = jnp.full(
                (1, width), ends[1 - side].astype(jnp.float32)
            )
        return carry

    lax.fori_loop(0, owned, place, 0, unroll=True)
    for copy in copies[4:]:
        copy.wait()


def face_parts(conduct, grid_size):
    rows, cols = conduct.shape
    row = lax.broadcasted_iota(jnp.int32, (rows, cols), 0) & (grid_size - 1)
    col = lax.broadcasted_iota(jnp.int32, (rows, cols), 1)
    below = jnp.where(row < grid_size - 1, (conduct + pltpu.roll(conduct, rows - 1, 0)) * 0.5, 0.0)
    above = jnp.where(row > 0, (conduct + pltpu.roll(conduct, 1, 0)) * 0.5, 0.0)
    right = jnp.where(col < cols - 1, (conduct + pltpu.roll(conduct, cols - 1, 1)) * 0.5, 0.0)
    left = jnp.where(col > 0, (conduct + pltpu.roll(conduct, 1, 1)) * 0.5, 0.0)
    return below, above, right, left


def split_pair(values):
    high_part = values.astype(jnp.bfloat16)
    low_part = (values - high_part.astype(jnp.float32)).astype(jnp.bfloat16)
    return high_part, low_part


def split_three(values):
    high_part, low_part = split_pair(values)
    rest = values - high_part.astype(jnp.float32) - low_part.astype(jnp.float32)
    return high_part, low_part, rest.astype(jnp.bfloat16)


def over_blocks(count_ref, blocks, work):
    per_block = count_ref.shape[0] // blocks
    work(0)
    if blocks > 1:
        needed = lax.div(count_ref[0, 0] + (per_block - 1), per_block)

        def step(block, carry):
            work(block)
            return carry

        lax.fori_loop(1, needed, step, 0)


def spread(row_hot_ref, col_hot_ref, total_ref, value_of, block):
    _, cols, lanes = col_hot_ref.shape
    group = 2
    width = value_of(block, 0).shape[1]
    total = None
    for start in range(0, lanes // width, group):
        parts = [[], []]
        for device in range(start, start + group):
            hot = col_hot_ref[block, :, device * width : (device + 1) * width]
            for part, value in zip(parts, split_pair(value_of(block, device)), strict=True):
                part.append(hot * value)
        right = jnp.concatenate([jnp.concatenate(part, axis=1) for part in parts], axis=0)
        product = lax.dot_general(
            row_hot_ref[block, :, start * width : (start + group) * width],
            right,
            (((1,), (1,)), ((), ())),
            preferred_element_type=jnp.float32,
        )
        total = product if total is None else total + product
    total = total[:, :cols] + total[:, cols:]
    if isinstance(block, int):
        total_ref[...] = total
    else:
        total_ref[...] += total


def gather(col_hot_ref, row_ref, peer_ref, both_ref, values_ref, block):
    _, per_block, width = row_ref.shape
    rows = both_ref.shape[0]
    group = 2
    row_ids = lax.broadcasted_iota(jnp.int32, (rows, width), 0)
    both = both_ref[...]
    for start in range(0, per_block, group):
        hot = col_hot_ref[block, :, start * width : (start + group) * width]
        picked = jnp.dot(both, jnp.concatenate([hot, hot], axis=0), preferred_element_type=jnp.float32)
        for offset in range(group):
            device = start + offset
            mine = picked[:, offset * width : (offset + 1) * width]
            hit = row_ids == row_ref[block, device : device + 1, :]
            values_ref[peer_ref[block, device, 0]] = jnp.sum(
                jnp.where(hit, mine, 0.0), axis=0, keepdims=True
            )


def send_values(adjoint, col_hot_ref, row_ref, count_ref, peer_ref, both_ref, values_ref):
    values_ref[...] = jnp.zeros(values_ref.shape, jnp.float32)
    both_ref[...] = jnp.concatenate(split_pair(adjoint), axis=1)
    over_blocks(
        count_ref, row_ref.shape[0],
        lambda block: gather(col_hot_ref, row_ref, peer_ref, both_ref, values_ref, block),
    )


def first_kernel(
    grid_size, message_ref, aperture_ref, source_hbm, pressure_hbm,
    values_ref, row_hot_ref, col_hot_ref, row_ref, weight_ref, count_ref, peer_ref, parts_ref, adjoint_ref,
    source_ref, pressure_ref, col_ref, total_ref, both_ref, sems,
):
    copies = start_copies(
        ((source_hbm, source_ref), (pressure_hbm, pressure_ref)), sems
    )
    devices, _, width = message_ref.shape
    trace_len = width // 2
    blocks, per_block, _ = col_ref.shape
    rows, cols = aperture_ref.shape
    aperture = aperture_ref[...]
    faces = face_parts(aperture * aperture * aperture / 12.0, grid_size)
    for index in range(4):
        parts_ref[index] = faces[index]
    parts_ref[4] = LEAKAGE + (faces[0] + faces[1] + faces[2] + faces[3])
    slots = [message_ref[:, rank, :] for rank in range(2)]
    partners = [message_ref[:, 2 + rank, :] for rank in range(2)]
    down = lax.broadcasted_iota(jnp.int32, (devices, width), 0)
    along = lax.broadcasted_iota(jnp.int32, (devices, width), 1)
    device_id = down.astype(jnp.float32)
    target = [
        jnp.sum(jnp.where(down == along, partners[rank], 0.0), axis=0, keepdims=True) for rank in range(2)
    ]
    target = [jnp.where(along[0:1] < devices, target[rank], -1.0) for rank in range(2)]
    used = jnp.where((device_id == target[0]) | (device_id == target[1]), 1.0, 0.0)
    used = jnp.max(used, axis=1, keepdims=True)
    count = jnp.sum(used, axis=0, keepdims=True)
    packed = jnp.zeros((2 * devices, 4 * width), jnp.float32)
    for rank in range(2):
        place = jnp.sum(jnp.where(device_id < target[rank], used, 0.0), axis=0, keepdims=True)
        ahead = (down < along) if rank == 0 else (down <= along)
        earlier = jnp.where((partners[0] == target[rank]) & ahead, 1.0, 0.0)
        earlier = earlier + jnp.where((partners[1] == target[rank]) & (down < along), 1.0, 0.0)
        spot = jnp.sum(earlier, axis=0, keepdims=True)
        here = (device_id == place) & (target[rank] >= 0.0)
        pick = [jnp.where(here & (spot == float(index)), 1.0, 0.0).astype(jnp.bfloat16) for index in range(2)]
        packed = packed + jnp.dot(
            jnp.concatenate(pick, axis=0)[:, :devices],
            jnp.concatenate(split_three(slots[rank]) + (partners[rank].astype(jnp.bfloat16),), axis=1),
            preferred_element_type=jnp.float32,
        )
    ends = packed[:, :width] + packed[:, width : 2 * width] + packed[:, 2 * width : 3 * width]
    ends = [ends[:devices], ends[devices:]]
    front = along < trace_len
    cell = jnp.where(front, ends[0], pltpu.roll(ends[1], trace_len, 1)).astype(jnp.int32) - 1
    weight = jnp.where(front, pltpu.roll(ends[0], trace_len, 1), ends[1])
    me = lax.axis_index(AXES)
    peer = jnp.where(device_id < count, packed[:devices, 3 * width :].astype(jnp.int32), me)
    count_ref[...] = jnp.broadcast_to(count, count_ref.shape).astype(jnp.int32)
    peer_ref[...] = peer.reshape(peer_ref.shape)
    weight_ref[...] = weight.reshape(weight_ref.shape)
    row_ref[...] = (cell >> (grid_size.bit_length() - 1)).reshape(row_ref.shape)
    col_ref[...] = (cell & (grid_size - 1)).reshape(col_ref.shape)
    cell_ids = lax.broadcasted_iota(jnp.int32, (rows, width), 0).astype(jnp.float32).astype(jnp.bfloat16)
    one, zero = jnp.ones((), jnp.bfloat16), jnp.zeros((), jnp.bfloat16)

    def build(block):
        block_cols = col_ref[block].astype(jnp.float32).astype(jnp.bfloat16)
        block_rows = row_ref[block].astype(jnp.float32).astype(jnp.bfloat16)
        for device in range(per_block):
            lanes = slice(device * width, (device + 1) * width)
            row_hot_ref[block, :, lanes] = jnp.where(cell_ids == block_rows[device : device + 1], one, zero)
            col_hot_ref[block, :, lanes] = jnp.where(
                cell_ids[:cols] == block_cols[device : device + 1], one, zero
            )
        spread(
            row_hot_ref, col_hot_ref, total_ref,
            lambda block, device: weight_ref[block, device : device + 1, :], block,
        )

    over_blocks(count_ref, blocks, build)
    inv_diag = 1.0 / (parts_ref[4] + total_ref[...])
    for copy in copies:
        copy.wait()
    parts_ref[4] = inv_diag
    adjoint = source_ref[...] * inv_diag
    adjoint_ref[...] = adjoint
    send_values(adjoint, col_hot_ref, row_ref, count_ref, peer_ref, both_ref, values_ref)


def near(state_ref, rows):
    cols = state_ref.shape[1]
    first = SLICE + rows
    here = state_ref[first : first + SLICE]
    return here, (
        state_ref[first + 1 : first + SLICE + 1],
        state_ref[first - 1 : first + SLICE - 1],
        pltpu.roll(here, cols - 1, 1),
        pltpu.roll(here, 1, 1),
    )


def relax(
    arrived_ref, row_hot_ref, col_hot_ref, weight_ref, count_ref, peer_ref, parts_ref, start_ref, source_ref,
    adjoint_ref, total_ref, early_ref, state_ref, scaled_ref, before_ref=None,
):
    rows, cols = start_ref.shape
    slices = range(0, rows, SLICE)
    margin = jnp.zeros((SLICE, cols), jnp.float32)
    for index in range(2):
        state_ref[index, 0:SLICE] = margin
        state_ref[index, SLICE + rows :] = margin
    state_ref[0, SLICE : SLICE + rows] = start_ref[...]

    def pull(state, first):
        _, (below, above, right, left) = near(state, first)
        here = slice(first, first + SLICE)
        return (scaled_ref[0, here] * below + scaled_ref[1, here] * above) + (
            scaled_ref[2, here] * right + scaled_ref[3, here] * left
        )

    for index in range(4):
        scaled_ref[index] = parts_ref[index] * parts_ref[4]
    for first in slices:
        early_ref[first : first + SLICE] = pull(state_ref.at[0], first)
    if before_ref is not None:
        before_ref()
    over_blocks(
        count_ref, weight_ref.shape[0],
        lambda block: spread(
            row_hot_ref, col_hot_ref, total_ref,
            lambda block, device: weight_ref[block, device : device + 1, :] * arrived_ref[peer_ref[block, device, 0]],
            block,
        ),
    )
    for step in range(INNER):
        old, new = state_ref.at[step % 2], state_ref.at[(step + 1) % 2]
        for first in slices:
            here = slice(first, first + SLICE)
            if step == 0:
                forcing = (source_ref[here] + total_ref[here]) * parts_ref[4, here]
                total_ref[here] = forcing
                now = forcing + early_ref[here]
            else:
                now = total_ref[here] + pull(old, first)
            new[SLICE + first : 2 * SLICE + first] = now
            if step == INNER - 1:
                adjoint_ref[here] = now


def sweep_kernel(
    arrived_ref, row_hot_ref, col_hot_ref, row_ref, weight_ref, count_ref, peer_ref, parts_ref, start_ref,
    source_ref, values_ref, adjoint_ref, total_ref, early_ref, state_ref, scaled_ref, both_ref,
):
    relax(
        arrived_ref, row_hot_ref, col_hot_ref, weight_ref, count_ref, peer_ref, parts_ref, start_ref, source_ref,
        adjoint_ref, total_ref, early_ref, state_ref, scaled_ref,
    )
    send_values(adjoint_ref[...], col_hot_ref, row_ref, count_ref, peer_ref, both_ref, values_ref)


def last_kernel(
    grid_size, arrived_ref, row_hot_ref, col_hot_ref, weight_ref, count_ref, peer_ref, parts_ref, start_ref,
    source_ref, aperture_ref, pressure_ref, gradient_hbm, adjoint_hbm,
    total_ref, early_ref, state_ref, scaled_ref, share_ref, gradient_ref, adjoint_ref, sems,
):
    rows, cols = start_ref.shape
    slices = range(0, rows, SLICE)

    def shares():
        aperture = aperture_ref[...]
        scale = -(aperture * aperture / 8.0)
        pressure = pressure_ref[...]
        row = lax.broadcasted_iota(jnp.int32, (rows, cols), 0) & (grid_size - 1)
        col = lax.broadcasted_iota(jnp.int32, (rows, cols), 1)
        inside = (row < grid_size - 1, row > 0, col < cols - 1, col > 0)
        turns = ((rows - 1, 0), (1, 0), (cols - 1, 1), (1, 1))
        for index in range(4):
            share_ref[index] = jnp.where(
                inside[index], scale * (pressure - pltpu.roll(pressure, *turns[index])), 0.0
            )

    relax(
        arrived_ref, row_hot_ref, col_hot_ref, weight_ref, count_ref, peer_ref, parts_ref, start_ref, source_ref,
        adjoint_ref, total_ref, early_ref, state_ref, scaled_ref, shares,
    )
    keep = pltpu.make_async_copy(adjoint_ref, adjoint_hbm, sems.at[0])
    keep.start()
    last_state = state_ref.at[INNER % 2]
    for first in slices:
        here, sides = near(last_state, first)
        lines = slice(first, first + SLICE)
        terms = [share_ref[index, lines] * (here - side) for index, side in enumerate(sides)]
        gradient_ref[lines] = (terms[0] + terms[1]) + (terms[2] + terms[3])
    send = pltpu.make_async_copy(gradient_ref, gradient_hbm, sems.at[1])
    send.start()
    keep.wait()
    send.wait()


def body(aperture, pressure, adj_source, trace_weight, end_device, end_local, trace_nodes):
    frac_count, grid_size, _ = aperture.shape
    owned_count, trace_len = trace_weight.shape
    device_count = lax.axis_size(AXES)
    rows, cols, width = frac_count * grid_size, grid_size, 2 * trace_len
    nodes = device_count * width
    per_block = math.gcd(device_count, 16)
    blocks = device_count // per_block
    in_vmem = pl.BlockSpec(memory_space=pltpu.VMEM)
    in_hbm = pl.BlockSpec(memory_space=pltpu.HBM)
    params = pltpu.CompilerParams(vmem_limit_bytes=(8 << 20) + nodes * 1024)
    field = pltpu.VMEM((rows, cols), jnp.float32)
    four = pltpu.VMEM((4, rows, cols), jnp.float32)
    sweeping = [field, field, pltpu.VMEM((2, rows + 2 * SLICE, cols), jnp.float32), four]
    leaving = [pltpu.VMEM((rows, 2 * cols), jnp.bfloat16)]
    ends_int = pltpu.VMEM((blocks, per_block, width), jnp.int32)
    ends_float = pltpu.VMEM((blocks, per_block, width), jnp.float32)

    def flat(whole):
        return whole.reshape(rows, cols)

    def vmem(*arrays):
        return [pltpu.with_memory_space_constraint(array, pltpu.VMEM) for array in arrays]

    def hbm(*arrays):
        return [pltpu.with_memory_space_constraint(array, pltpu.HBM) for array in arrays]

    def exchange(values):
        return lax.all_to_all(values, AXES, split_axis=0, concat_axis=0, tiled=True)

    message, aperture_here = pl.pallas_call(
        functools.partial(pack_kernel, grid_size * grid_size),
        out_shape=[pltpu.VMEM((device_count, 4, width), jnp.float32), field],
        in_specs=[in_hbm] * 5,
        out_specs=[in_vmem] * 2,
        scratch_shapes=[
            pltpu.SMEM((2, owned_count), jnp.int32),
            pltpu.SMEM((2, owned_count), jnp.int32),
            pltpu.VMEM(trace_nodes.shape, jnp.int32),
            pltpu.VMEM(trace_weight.shape, jnp.float32),
            pltpu.SMEM((device_count,), jnp.int32),
            pltpu.SemaphoreType.DMA((8,)),
        ],
        compiler_params=params,
        name="pack_ends",
    )(*hbm(end_device.T, end_local.T, trace_nodes, trace_weight, flat(aperture)))
    values_shape = pltpu.VMEM((device_count, 1, width), jnp.float32)
    (
        values, row_hot, col_hot, row, weight, count, peer, parts, adjoint, source_here, pressure_here,
    ) = pl.pallas_call(
        functools.partial(first_kernel, grid_size),
        out_shape=[
            values_shape,
            pltpu.VMEM((blocks, rows, per_block * width), jnp.bfloat16),
            pltpu.VMEM((blocks, cols, per_block * width), jnp.bfloat16),
            ends_int,
            ends_float,
            pltpu.VMEM((device_count, width), jnp.int32),
            ends_int,
            pltpu.VMEM((5, rows, cols), jnp.float32),
        ]
        + [field] * 3,
        in_specs=[in_vmem] * 2 + [in_hbm] * 2,
        out_specs=[in_vmem] * 11,
        scratch_shapes=[ends_int, field] + leaving + [pltpu.SemaphoreType.DMA((2,))],
        compiler_params=params,
        name="first_values",
    )(*vmem(exchange(message), aperture_here), *hbm(flat(adj_source), flat(pressure)))
    for _ in range(SWEEPS - 1):
        values, adjoint = pl.pallas_call(
            sweep_kernel,
            out_shape=[values_shape, field],
            in_specs=[in_vmem] * 10,
            out_specs=[in_vmem] * 2,
            scratch_shapes=sweeping + leaving,
            compiler_params=params,
            name="sweep",
        )(
            *vmem(
                exchange(values), row_hot, col_hot, row, weight, count, peer, parts, adjoint, source_here
            )
        )
    gradient, adjoint = pl.pallas_call(
        functools.partial(last_kernel, grid_size),
        out_shape=[jax.ShapeDtypeStruct((rows, cols), jnp.float32)] * 2,
        in_specs=[in_vmem] * 11,
        out_specs=[in_hbm] * 2,
        scratch_shapes=sweeping
        + [pltpu.VMEM((4, rows, cols), jnp.float32), field, field, pltpu.SemaphoreType.DMA((2,))],
        compiler_params=params,
        name="last_sweep",
    )(
        *vmem(
            exchange(values), row_hot, col_hot, weight, count, peer, parts, adjoint,
            source_here, aperture_here, pressure_here,
        )
    )
    return gradient.reshape(aperture.shape), adjoint.reshape(aperture.shape)


def solution(mesh):
    fields, pairs = P(AXES, None, None), P(AXES, None)
    return jax.shard_map(
        body,
        mesh=mesh,
        in_specs=(fields, fields, fields, pairs, pairs, pairs, fields),
        out_specs=(fields, fields),
        check_vma=False,
    )
```

```python
import functools
import math

import jax
import jax.numpy as jnp
from jax import lax
from jax.experimental import pallas as pl
from jax.experimental.pallas import tpu as pltpu
from jax.sharding import PartitionSpec as P

SWEEPS = 3
INNER = 8
LEAKAGE = 0.25
AXES = ("wide", "narrow")
SLICE = 8


def start_copies(pairs, sems):
    copies = [
        pltpu.make_async_copy(source, target, sems.at[index]) for index, (source, target) in enumerate(pairs)
    ]
    for copy in copies:
        copy.start()
    return copies


def pack_kernel(
    cells_per, dest_hbm, local_hbm, nodes_hbm, weight_hbm, aperture_hbm,
    out_ref, aperture_ref, dest_ref, local_ref, nodes_ref, weight_ref, seen_ref, sems,
):
    owned = nodes_ref.shape[0]
    devices, _, width = out_ref.shape
    rows = aperture_ref.shape[0]
    copies = start_copies(
        (
            (dest_hbm, dest_ref), (local_hbm, local_ref), (nodes_hbm, nodes_ref), (weight_hbm, weight_ref),
        )
        + tuple(
            (aperture_hbm.at[pl.ds(first, rows // 4)], aperture_ref.at[pl.ds(first, rows // 4)])
            for first in range(0, rows, rows // 4)
        ),
        sems,
    )

    def clear(device, carry):
        seen_ref[device] = 0
        return carry

    lax.fori_loop(0, devices, clear, 0, unroll=8)
    out_ref[:, 0:2, :] = jnp.zeros((devices, 2, width), jnp.float32)
    out_ref[:, 2:4, :] = jnp.full((devices, 2, width), -1.0, jnp.float32)
    for copy in copies[:4]:
        copy.wait()

    def place(index, carry):
        ends = [dest_ref[0, index], dest_ref[1, index]]
        weights = weight_ref[pl.ds(index, 1), :]
        for side in range(2):
            target = ends[side]
            rank = seen_ref[target]
            seen_ref[target] = rank + 1
            first = local_ref[side, index] * cells_per + 1
            cells = (nodes_ref[index, side : side + 1, :] + first).astype(jnp.float32)
            out_ref[target, pl.ds(rank, 1), :] = jnp.concatenate([cells, weights], axis=1)
            out_ref[target, pl.ds(rank + 2, 1), :] = jnp.full(
                (1, width), ends[1 - side].astype(jnp.float32)
            )
        return carry

    lax.fori_loop(0, owned, place, 0, unroll=True)
    for copy in copies[4:]:
        copy.wait()


def face_parts(conduct, grid_size):
    rows, cols = conduct.shape
    row = lax.broadcasted_iota(jnp.int32, (rows, cols), 0) & (grid_size - 1)
    col = lax.broadcasted_iota(jnp.int32, (rows, cols), 1)
    below = jnp.where(row < grid_size - 1, (conduct + pltpu.roll(conduct, rows - 1, 0)) * 0.5, 0.0)
    above = jnp.where(row > 0, (conduct + pltpu.roll(conduct, 1, 0)) * 0.5, 0.0)
    right = jnp.where(col < cols - 1, (conduct + pltpu.roll(conduct, cols - 1, 1)) * 0.5, 0.0)
    left = jnp.where(col > 0, (conduct + pltpu.roll(conduct, 1, 1)) * 0.5, 0.0)
    return below, above, right, left


def split_pair(values):
    high_part = values.astype(jnp.bfloat16)
    low_part = (values - high_part.astype(jnp.float32)).astype(jnp.bfloat16)
    return high_part, low_part


def split_three(values):
    high_part, low_part = split_pair(values)
    rest = values - high_part.astype(jnp.float32) - low_part.astype(jnp.float32)
    return high_part, low_part, rest.astype(jnp.bfloat16)


def over_blocks(count_ref, blocks, work):
    per_block = count_ref.shape[0] // blocks
    work(0)
    if blocks > 1:
        needed = lax.div(count_ref[0, 0] + (per_block - 1), per_block)

        def step(block, carry):
            work(block)
            return carry

        lax.fori_loop(1, needed, step, 0)


def spread(row_hot_ref, col_hot_ref, total_ref, value_of, block):
    _, cols, lanes = col_hot_ref.shape
    group = 2
    width = value_of(block, 0).shape[1]
    total = None
    for start in range(0, lanes // width, group):
        parts = [[], []]
        for device in range(start, start + group):
            hot = col_hot_ref[block, :, device * width : (device + 1) * width]
            for part, value in zip(parts, split_pair(value_of(block, device)), strict=True):
                part.append(hot * value)
        right = jnp.concatenate([jnp.concatenate(part, axis=1) for part in parts], axis=0)
        product = lax.dot_general(
            row_hot_ref[block, :, start * width : (start + group) * width],
            right,
            (((1,), (1,)), ((), ())),
            preferred_element_type=jnp.float32,
        )
        total = product if total is None else total + product
    total = total[:, :cols] + total[:, cols:]
    if isinstance(block, int):
        total_ref[...] = total
    else:
        total_ref[...] += total


def gather(col_hot_ref, row_ref, peer_ref, both_ref, values_ref, block):
    _, per_block, width = row_ref.shape
    rows = both_ref.shape[0]
    group = 4
    row_ids = lax.broadcasted_iota(jnp.int32, (rows, width), 0)
    both = both_ref[...]
    for start in range(0, per_block, group):
        hot = col_hot_ref[block, :, start * width : (start + group) * width]
        picked = jnp.dot(both, jnp.concatenate([hot, hot], axis=0), preferred_element_type=jnp.float32)
        for offset in range(group):
            device = start + offset
            mine = picked[:, offset * width : (offset + 1) * width]
            hit = row_ids == row_ref[block, device : device + 1, :]
            values_ref[peer_ref[block, device, 0]] = jnp.sum(
                jnp.where(hit, mine, 0.0), axis=0, keepdims=True
            )


def send_values(adjoint, col_hot_ref, row_ref, count_ref, peer_ref, both_ref, values_ref):
    values_ref[...] = jnp.zeros(values_ref.shape, jnp.float32)
    both_ref[...] = jnp.concatenate(split_pair(adjoint), axis=1)
    over_blocks(
        count_ref, row_ref.shape[0],
        lambda block: gather(col_hot_ref, row_ref, peer_ref, both_ref, values_ref, block),
    )


def first_kernel(
    grid_size, message_ref, aperture_ref, source_hbm, pressure_hbm,
    values_ref, row_hot_ref, col_hot_ref, row_ref, weight_ref, count_ref, peer_ref, parts_ref, adjoint_ref,
    source_ref, pressure_ref, col_ref, total_ref, both_ref, sems,
):
    copies = start_copies(
        ((source_hbm, source_ref), (pressure_hbm, pressure_ref)), sems
    )
    devices, _, width = message_ref.shape
    trace_len = width // 2
    blocks, per_block, _ = col_ref.shape
    rows, cols = aperture_ref.shape
    aperture = aperture_ref[...]
    faces = face_parts(aperture * aperture * aperture / 12.0, grid_size)
    for index in range(4):
        parts_ref[index] = faces[index]
    parts_ref[4] = LEAKAGE + (faces[0] + faces[1] + faces[2] + faces[3])
    slots = [message_ref[:, rank, :] for rank in range(2)]
    partners = [message_ref[:, 2 + rank, :] for rank in range(2)]
    down = lax.broadcasted_iota(jnp.int32, (devices, width), 0)
    along = lax.broadcasted_iota(jnp.int32, (devices, width), 1)
    device_id = down.astype(jnp.float32)
    target = [
        jnp.sum(jnp.where(down == along, partners[rank], 0.0), axis=0, keepdims=True) for rank in range(2)
    ]
    target = [jnp.where(along[0:1] < devices, target[rank], -1.0) for rank in range(2)]
    used = jnp.where((device_id == target[0]) | (device_id == target[1]), 1.0, 0.0)
    used = jnp.max(used, axis=1, keepdims=True)
    count = jnp.sum(used, axis=0, keepdims=True)
    packed = jnp.zeros((2 * devices, 4 * width), jnp.float32)
    for rank in range(2):
        place = jnp.sum(jnp.where(device_id < target[rank], used, 0.0), axis=0, keepdims=True)
        ahead = (down < along) if rank == 0 else (down <= along)
        earlier = jnp.where((partners[0] == target[rank]) & ahead, 1.0, 0.0)
        earlier = earlier + jnp.where((partners[1] == target[rank]) & (down < along), 1.0, 0.0)
        spot = jnp.sum(earlier, axis=0, keepdims=True)
        here = (device_id == place) & (target[rank] >= 0.0)
        pick = [jnp.where(here & (spot == float(index)), 1.0, 0.0).astype(jnp.bfloat16) for index in range(2)]
        packed = packed + jnp.dot(
            jnp.concatenate(pick, axis=0)[:, :devices],
            jnp.concatenate(split_three(slots[rank]) + (partners[rank].astype(jnp.bfloat16),), axis=1),
            preferred_element_type=jnp.float32,
        )
    ends = packed[:, :width] + packed[:, width : 2 * width] + packed[:, 2 * width : 3 * width]
    ends = [ends[:devices], ends[devices:]]
    front = along < trace_len
    cell = jnp.where(front, ends[0], pltpu.roll(ends[1], trace_len, 1)).astype(jnp.int32) - 1
    weight = jnp.where(front, pltpu.roll(ends[0], trace_len, 1), ends[1])
    me = lax.axis_index(AXES)
    peer = jnp.where(device_id < count, packed[:devices, 3 * width :].astype(jnp.int32), me)
    count_ref[...] = jnp.broadcast_to(count, count_ref.shape).astype(jnp.int32)
    peer_ref[...] = peer.reshape(peer_ref.shape)
    weight_ref[...] = weight.reshape(weight_ref.shape)
    row_ref[...] = (cell >> (grid_size.bit_length() - 1)).reshape(row_ref.shape)
    col_ref[...] = (cell & (grid_size - 1)).reshape(col_ref.shape)
    cell_ids = lax.broadcasted_iota(jnp.int32, (rows, width), 0).astype(jnp.float32).astype(jnp.bfloat16)
    one, zero = jnp.ones((), jnp.bfloat16), jnp.zeros((), jnp.bfloat16)

    def build(block):
        block_cols = col_ref[block].astype(jnp.float32).astype(jnp.bfloat16)
        block_rows = row_ref[block].astype(jnp.float32).astype(jnp.bfloat16)
        for device in range(per_block):
            lanes = slice(device * width, (device + 1) * width)
            row_hot_ref[block, :, lanes] = jnp.where(cell_ids == block_rows[device : device + 1], one, zero)
            col_hot_ref[block, :, lanes] = jnp.where(
                cell_ids[:cols] == block_cols[device : device + 1], one, zero
            )
        spread(
            row_hot_ref, col_hot_ref, total_ref,
            lambda block, device: weight_ref[block, device : device + 1, :], block,
        )

    over_blocks(count_ref, blocks, build)
    inv_diag = 1.0 / (parts_ref[4] + total_ref[...])
    for copy in copies:
        copy.wait()
    parts_ref[4] = inv_diag
    adjoint = source_ref[...] * inv_diag
    adjoint_ref[...] = adjoint
    send_values(adjoint, col_hot_ref, row_ref, count_ref, peer_ref, both_ref, values_ref)


def near(state_ref, rows):
    cols = state_ref.shape[1]
    first = SLICE + rows
    here = state_ref[first : first + SLICE]
    return here, (
        state_ref[first + 1 : first + SLICE + 1],
        state_ref[first - 1 : first + SLICE - 1],
        pltpu.roll(here, cols - 1, 1),
        pltpu.roll(here, 1, 1),
    )


def relax(
    arrived_ref, row_hot_ref, col_hot_ref, weight_ref, count_ref, peer_ref, parts_ref, start_ref, source_ref,
    adjoint_ref, total_ref, early_ref, state_ref, before_ref=None,
):
    rows, cols = start_ref.shape
    slices = range(0, rows, SLICE)
    margin = jnp.zeros((SLICE, cols), jnp.float32)
    for index in range(2):
        state_ref[index, 0:SLICE] = margin
        state_ref[index, SLICE + rows :] = margin
    state_ref[0, SLICE : SLICE + rows] = start_ref[...]

    def pull(state, first):
        _, (below, above, right, left) = near(state, first)
        here = slice(first, first + SLICE)
        return (parts_ref[0, here] * below + parts_ref[1, here] * above) + (
            parts_ref[2, here] * right + parts_ref[3, here] * left
        )

    for first in slices:
        early_ref[first : first + SLICE] = pull(state_ref.at[0], first)
    if before_ref is not None:
        before_ref()
    over_blocks(
        count_ref, weight_ref.shape[0],
        lambda block: spread(
            row_hot_ref, col_hot_ref, total_ref,
            lambda block, device: weight_ref[block, device : device + 1, :] * arrived_ref[peer_ref[block, device, 0]],
            block,
        ),
    )
    for step in range(INNER):
        old, new = state_ref.at[step % 2], state_ref.at[(step + 1) % 2]
        for first in slices:
            here = slice(first, first + SLICE)
            if step == 0:
                forcing = source_ref[here] + total_ref[here]
                total_ref[here] = forcing
                now = (forcing + early_ref[here]) * parts_ref[4, here]
            else:
                now = (total_ref[here] + pull(old, first)) * parts_ref[4, here]
            new[SLICE + first : 2 * SLICE + first] = now
            if step == INNER - 1:
                adjoint_ref[here] = now


def sweep_kernel(
    arrived_ref, row_hot_ref, col_hot_ref, row_ref, weight_ref, count_ref, peer_ref, parts_ref, start_ref,
    source_ref, values_ref, adjoint_ref, total_ref, early_ref, state_ref, both_ref,
):
    relax(
        arrived_ref, row_hot_ref, col_hot_ref, weight_ref, count_ref, peer_ref, parts_ref, start_ref, source_ref,
        adjoint_ref, total_ref, early_ref, state_ref,
    )
    send_values(adjoint_ref[...], col_hot_ref, row_ref, count_ref, peer_ref, both_ref, values_ref)


def last_kernel(
    grid_size, arrived_ref, row_hot_ref, col_hot_ref, weight_ref, count_ref, peer_ref, parts_ref, start_ref,
    source_ref, aperture_ref, pressure_ref, gradient_hbm, adjoint_hbm,
    total_ref, early_ref, state_ref, share_ref, gradient_ref, adjoint_ref, sems,
):
    rows, cols = start_ref.shape
    slices = range(0, rows, SLICE)

    def shares():
        aperture = aperture_ref[...]
        scale = -(aperture * aperture / 8.0)
        pressure = pressure_ref[...]
        row = lax.broadcasted_iota(jnp.int32, (rows, cols), 0) & (grid_size - 1)
        col = lax.broadcasted_iota(jnp.int32, (rows, cols), 1)
        inside = (row < grid_size - 1, row > 0, col < cols - 1, col > 0)
        turns = ((rows - 1, 0), (1, 0), (cols - 1, 1), (1, 1))
        for index in range(4):
            share_ref[index] = jnp.where(
                inside[index], scale * (pressure - pltpu.roll(pressure, *turns[index])), 0.0
            )

    relax(
        arrived_ref, row_hot_ref, col_hot_ref, weight_ref, count_ref, peer_ref, parts_ref, start_ref, source_ref,
        adjoint_ref, total_ref, early_ref, state_ref, shares,
    )
    keep = pltpu.make_async_copy(adjoint_ref, adjoint_hbm, sems.at[0])
    keep.start()
    last_state = state_ref.at[INNER % 2]
    for first in slices:
        here, sides = near(last_state, first)
        lines = slice(first, first + SLICE)
        terms = [share_ref[index, lines] * (here - side) for index, side in enumerate(sides)]
        gradient_ref[lines] = (terms[0] + terms[1]) + (terms[2] + terms[3])
    send = pltpu.make_async_copy(gradient_ref, gradient_hbm, sems.at[1])
    send.start()
    keep.wait()
    send.wait()


def body(aperture, pressure, adj_source, trace_weight, end_device, end_local, trace_nodes):
    frac_count, grid_size, _ = aperture.shape
    owned_count, trace_len = trace_weight.shape
    device_count = lax.axis_size(AXES)
    rows, cols, width = frac_count * grid_size, grid_size, 2 * trace_len
    nodes = device_count * width
    per_block = math.gcd(device_count, 16)
    blocks = device_count // per_block
    in_vmem = pl.BlockSpec(memory_space=pltpu.VMEM)
    in_hbm = pl.BlockSpec(memory_space=pltpu.HBM)
    params = pltpu.CompilerParams(vmem_limit_bytes=(8 << 20) + nodes * 1024)
    field = pltpu.VMEM((rows, cols), jnp.float32)
    sweeping = [field, field, pltpu.VMEM((2, rows + 2 * SLICE, cols), jnp.float32)]
    leaving = [pltpu.VMEM((rows, 2 * cols), jnp.bfloat16)]
    ends_int = pltpu.VMEM((blocks, per_block, width), jnp.int32)
    ends_float = pltpu.VMEM((blocks, per_block, width), jnp.float32)

    def flat(whole):
        return whole.reshape(rows, cols)

    def vmem(*arrays):
        return [pltpu.with_memory_space_constraint(array, pltpu.VMEM) for array in arrays]

    def hbm(*arrays):
        return [pltpu.with_memory_space_constraint(array, pltpu.HBM) for array in arrays]

    def exchange(values):
        return lax.all_to_all(values, AXES, split_axis=0, concat_axis=0, tiled=True)

    message, aperture_here = pl.pallas_call(
        functools.partial(pack_kernel, grid_size * grid_size),
        out_shape=[pltpu.VMEM((device_count, 4, width), jnp.float32), field],
        in_specs=[in_hbm] * 5,
        out_specs=[in_vmem] * 2,
        scratch_shapes=[
            pltpu.SMEM((2, owned_count), jnp.int32),
            pltpu.SMEM((2, owned_count), jnp.int32),
            pltpu.VMEM(trace_nodes.shape, jnp.int32),
            pltpu.VMEM(trace_weight.shape, jnp.float32),
            pltpu.SMEM((device_count,), jnp.int32),
            pltpu.SemaphoreType.DMA((8,)),
        ],
        compiler_params=params,
        name="pack_ends",
    )(*hbm(end_device.T, end_local.T, trace_nodes, trace_weight, flat(aperture)))
    values_shape = pltpu.VMEM((device_count, 1, width), jnp.float32)
    (
        values, row_hot, col_hot, row, weight, count, peer, parts, adjoint, source_here, pressure_here,
    ) = pl.pallas_call(
        functools.partial(first_kernel, grid_size),
        out_shape=[
            values_shape,
            pltpu.VMEM((blocks, rows, per_block * width), jnp.bfloat16),
            pltpu.VMEM((blocks, cols, per_block * width), jnp.bfloat16),
            ends_int,
            ends_float,
            pltpu.VMEM((device_count, width), jnp.int32),
            ends_int,
            pltpu.VMEM((5, rows, cols), jnp.float32),
        ]
        + [field] * 3,
        in_specs=[in_vmem] * 2 + [in_hbm] * 2,
        out_specs=[in_vmem] * 11,
        scratch_shapes=[ends_int, field] + leaving + [pltpu.SemaphoreType.DMA((2,))],
        compiler_params=params,
        name="first_values",
    )(*vmem(exchange(message), aperture_here), *hbm(flat(adj_source), flat(pressure)))
    for _ in range(SWEEPS - 1):
        values, adjoint = pl.pallas_call(
            sweep_kernel,
            out_shape=[values_shape, field],
            in_specs=[in_vmem] * 10,
            out_specs=[in_vmem] * 2,
            scratch_shapes=sweeping + leaving,
            compiler_params=params,
            name="sweep",
        )(
            *vmem(
                exchange(values), row_hot, col_hot, row, weight, count, peer, parts, adjoint, source_here
            )
        )
    gradient, adjoint = pl.pallas_call(
        functools.partial(last_kernel, grid_size),
        out_shape=[jax.ShapeDtypeStruct((rows, cols), jnp.float32)] * 2,
        in_specs=[in_vmem] * 11,
        out_specs=[in_hbm] * 2,
        scratch_shapes=sweeping
        + [pltpu.VMEM((4, rows, cols), jnp.float32), field, field, pltpu.SemaphoreType.DMA((2,))],
        compiler_params=params,
        name="last_sweep",
    )(
        *vmem(
            exchange(values), row_hot, col_hot, weight, count, peer, parts, adjoint,
            source_here, aperture_here, pressure_here,
        )
    )
    return gradient.reshape(aperture.shape), adjoint.reshape(aperture.shape)


def solution(mesh):
    fields, pairs = P(AXES, None, None), P(AXES, None)
    return jax.shard_map(
        body,
        mesh=mesh,
        in_specs=(fields, fields, fields, pairs, pairs, pairs, fields),
        out_specs=(fields, fields),
        check_vma=False,
    )
```
